512 devices in a mesh: gx: 32 (over y, x), yz: 16 (over z, core).
Axes of the slice: x: 4, y: 8, z: 8, core: 2. Of those that a mesh axis runs over, the one named last changes fastest.
Arguments:
- right_side: float32 [32, 16, 80, 768], P('gx', 'yz'), may hold values from -750 to 750
- face_table: int32 [32, 16, 4, 512], P('gx', 'yz'), may hold values from 0 to 1023, as said below
- send_faces: int32 [32, 16, 2, 128], P('gx', 'yz'), may hold values from 0 to 767, as said below
- stabilize: float32 [32, 16, 512], P('gx', 'yz'), may hold values from 3 to 6
- coupling: float32 [32, 16, 512], P('gx', 'yz'), may hold values from 0.5 to 2
- inverse: float32 [2, 192, 192], replicated, may hold values from -0.4375 to 0.4375
- lifting: float32 [2, 320, 192], replicated, may hold values from -0.3125 to 0.3125
- trace_block: float32 [2, 320, 320], replicated, may hold values from -0.3125 to 0.3125
Outputs:
- solution: float32 [32, 16, 80, 768], P('gx', 'yz')
The draws below stay inside these ranges and needn't reach their ends.
Inputs may be any that keep to these rules, and one draw needn't show every extreme that they name: `face_table`: on each device every local face 0 to 1023 appears exactly twice. Local faces below 768 are the device's own, the next 128 are the faces in row 0 of send_faces of the previous device along gx, in that order, and the last 128 those in row 1 of the previous device along yz. `send_faces`: on each device the 256 entries are distinct.
All inputs are finite; a program needn't handle non-finite values.
Results may differ from the reference program's by a relative error of at most 0.003.
Values sent between devices are 32-bit elements; how exact they have to be, the bound alone decides.
No kernel may reach another device: no remote copies, remote signals or barrier semaphores. Data moves between devices by JAX's collectives and lax.ppermute only.
A program may use at most 64 MiB of HBM per device.

```python
import math
import jax
import jax.numpy as jnp
from jax import lax

DOF = 80
INNER = 192
TYPES = 2
ITERS = 4
ELEM_DEV = 512
TRACE = 320
SHARED = 128
OWNED = 768
FACE_EXT = 1024
SLABS = 32
SECTS = 16


def draw_right_side(key, part):
    key = jax.random.fold_in(key, 11)
    keys = jax.random.split(key, 3)
    shape = (SLABS, SECTS, DOF, OWNED)
    base = jnp.clip(jax.random.normal(keys[0], shape, jnp.float32), -4.0, 4.0)
    climb = 3.0
    row_scale = jnp.exp(jax.random.uniform(keys[1], (SLABS, SECTS, DOF, 1), jnp.float32, 0.0, math.log(10.0)))
    column_scale = jnp.exp(jax.random.uniform(keys[2], (SLABS, SECTS, 1, OWNED), jnp.float32, 0.0, math.log(10.0)))
    position = jnp.arange(SLABS * SECTS, dtype=jnp.float32).reshape(SLABS, SECTS, 1, 1) / max(SLABS * SECTS - 1, 1)
    rising = climb ** position
    return 0.3 * base * row_scale * column_scale * rising


def draw_face_table(key, part):
    key = jax.random.fold_in(key, 23)
    keys = jax.random.split(key, SLABS * SECTS)
    listing = jnp.tile(jnp.arange(FACE_EXT, dtype=jnp.int32), 2)
    shuffled = jax.vmap(lambda single: jax.random.permutation(single, listing))(keys)
    return shuffled.astype(jnp.int32).reshape(SLABS, SECTS, 4, ELEM_DEV)


def pick_faces(single):
    first, second = jax.random.split(single)
    middle = jax.random.permutation(first, OWNED - 2)[:2 * SHARED - 2].astype(jnp.int32) + 1
    ends = jnp.array([0, OWNED - 1], dtype=jnp.int32)
    joined = jnp.concatenate([ends, middle])
    return jax.random.permutation(second, joined).astype(jnp.int32)


def draw_send_faces(key, part):
    key = jax.random.fold_in(key, 37)
    keys = jax.random.split(key, SLABS * SECTS)
    picked = jax.vmap(pick_faces)(keys)
    return picked.reshape(SLABS, SECTS, 2, SHARED)


def shard_levels(stream_key, shape, cuts, low, top_value):
    gain = 1.0
    for dim, blocks in cuts:
        draws = jax.random.uniform(jax.random.fold_in(jax.random.fold_in(stream_key, 6), dim), (blocks,), jnp.float32, low / len(cuts), top_value / len(cuts))
        gain = gain * jnp.repeat(jnp.exp(draws), shape[dim] // blocks).reshape((-1,) + (1,) * (len(shape) - 1 - dim))
    return gain


def bell_draw(own_key, shape, deviation, limit, kind=jnp.bfloat16):
    drawn = deviation * jax.random.normal(own_key, shape, jnp.float32)
    return jnp.clip(drawn, min=-limit, max=limit).astype(kind)


def setup_inputs(seed: int = 0) -> dict:
    splits = jax.random.split(jax.random.key(seed), 9)
    right_side = draw_right_side(jax.random.fold_in(splits[8], 71), 0)
    face_table = draw_face_table(jax.random.fold_in(splits[8], 71), 0)
    send_faces = draw_send_faces(jax.random.fold_in(splits[8], 71), 0)
    stabilize = jnp.clip(jnp.exp(math.log(6.0) - 0.6931472 * jax.random.uniform(splits[3], (SLABS, SECTS, ELEM_DEV), jnp.float32) ** shard_levels(splits[3], (SLABS, SECTS, ELEM_DEV), ((0, 32), (1, 16)), -0.2, 0.2)), 3.0, 6.0)
    coupling = jnp.clip(jnp.exp(math.log(2.0) - 1.3862944 * jax.random.uniform(splits[4], (SLABS, SECTS, ELEM_DEV), jnp.float32) ** shard_levels(splits[4], (SLABS, SECTS, ELEM_DEV), ((0, 32), (1, 16)), -0.2, 0.2)), 0.5, 2.0)
    inverse = bell_draw(splits[5], (TYPES, INNER, INNER), INNER ** -0.5, 0.4375, jnp.float32)
    lifting = bell_draw(splits[6], (TYPES, TRACE, INNER), TRACE ** -0.5, 0.3125, jnp.float32)
    trace_block = bell_draw(splits[7], (TYPES, TRACE, TRACE), TRACE ** -0.5, 0.3125, jnp.float32)
    return {"right_side": right_side, "face_table": face_table, "send_faces": send_faces, "stabilize": stabilize, "coupling": coupling, "inverse": inverse, "lifting": lifting, "trace_block": trace_block}


EPSILON = 1e-06

def element_apply(extended, element_faces, penalty, scaling, inverse, lifting, trace_block):
    trace_dofs = extended.shape[0]
    elements = element_faces.shape[1]
    shapes = lifting.shape[0]
    group = elements // shapes
    gathered = extended[:, element_faces].reshape(trace_dofs * 4, shapes, group)
    penalty_grid = penalty.reshape(shapes, group)
    scaling_grid = scaling.reshape(shapes, group)
    interior = jnp.einsum('kji,jkn->ikn', lifting, gathered, precision=lax.Precision.HIGHEST)
    solved = jnp.einsum('kmi,mkn->ikn', inverse, interior, precision=lax.Precision.HIGHEST) / scaling_grid
    result = penalty_grid * gathered + jnp.einsum('kji,jkn->ikn', trace_block, gathered, precision=lax.Precision.HIGHEST)
    result = result - jnp.einsum('kji,ikn->jkn', lifting, solved, precision=lax.Precision.HIGHEST)
    result = result.reshape(trace_dofs, 4, elements)
    return jnp.zeros(extended.shape, jnp.float32).at[:, element_faces].add(result)

def least_squares(hessenberg, target):
    breadth = hessenberg.shape[1]
    unit_columns = []
    triangle = {}
    for k in range(breadth):
        column = hessenberg[:, k]
        for i in range(k):
            triangle[i, k] = jnp.sum(unit_columns[i] * column)
            column = column - triangle[i, k] * unit_columns[i]
        triangle[k, k] = jnp.sqrt(jnp.sum(column * column))
        unit_columns.append(column / triangle[k, k])
    projected = [jnp.sum(vector * target) for vector in unit_columns]
    outcome = [None] * breadth
    for k in reversed(range(breadth)):
        running = projected[k]
        for i in range(k + 1, breadth):
            running = running - triangle[k, i] * outcome[i]
        outcome[k] = running / triangle[k, k]
    return outcome

def reference(right_side, face_table, send_faces, stabilize, coupling, inverse, lifting, trace_block):
    devices = SLABS * SECTS
    take_columns = jax.vmap(jax.vmap(lambda field, index: field[:, index]))
    add_columns = jax.vmap(jax.vmap(lambda field, index, extra: field.at[:, index].add(extra)))
    flat_faces = face_table.reshape(devices, 4, ELEM_DEV)
    flat_penalty = stabilize.reshape(devices, ELEM_DEV)
    flat_scaling = coupling.reshape(devices, ELEM_DEV)

    def one_device(items):
        extended, element_faces, penalty, scaling = items
        return element_apply(extended, element_faces, penalty, scaling, inverse, lifting, trace_block)

    def operator(vector):
        slab_ghost = jnp.roll(take_columns(vector, send_faces[:, :, 0]), 1, axis=0)
        section_ghost = jnp.roll(take_columns(vector, send_faces[:, :, 1]), 1, axis=1)
        extended = jnp.concatenate([vector, slab_ghost, section_ghost], axis=-1)
        summed = lax.map(one_device, (extended.reshape(devices, DOF, FACE_EXT), flat_faces, flat_penalty, flat_scaling))
        summed = summed.reshape(SLABS, SECTS, DOF, FACE_EXT)
        owned_part = summed[..., :OWNED]
        from_slab = jnp.roll(summed[..., OWNED:OWNED + SHARED], -1, axis=0)
        from_section = jnp.roll(summed[..., OWNED + SHARED:], -1, axis=1)
        owned_part = add_columns(owned_part, send_faces[:, :, 0], from_slab)
        return add_columns(owned_part, send_faces[:, :, 1], from_section)
    initial_norm = jnp.sqrt(jnp.sum(right_side * right_side) + EPSILON)
    krylov = [right_side / initial_norm]
    hessenberg = jnp.zeros((ITERS + 1, ITERS), jnp.float32)
    for j in range(ITERS):
        fresh = operator(krylov[j])
        products = jnp.stack([jnp.sum(krylov[i] * fresh) for i in range(j + 1)])
        for i in range(j + 1):
            fresh = fresh - products[i] * krylov[i]
        subdiag = jnp.sqrt(jnp.sum(fresh * fresh) + EPSILON)
        hessenberg = hessenberg.at[:j + 1, j].set(products).at[j + 1, j].set(subdiag)
        krylov.append(fresh / subdiag)
    target = jnp.zeros((ITERS + 1,), jnp.float32).at[0].set(initial_norm)
    combine = least_squares(hessenberg, target)
    solution = combine[0] * krylov[0]
    for j in range(1, ITERS):
        solution = solution + combine[j] * krylov[j]
    return solution
```

```python
import functools

import jax
import jax.numpy as jnp
from jax import lax
from jax.experimental import pallas as pl
from jax.experimental.pallas import tpu as pltpu
from jax.sharding import PartitionSpec as P

ITERS = 4
EPSILON = 1e-06
SHIFT = 12.0
NORM_ROOM = 1024.0
F32 = jnp.float32
BF16 = jnp.bfloat16
PAIRS = [(i, j) for j in range(ITERS + 1) for i in range(j + 1)]
VMEM_BYTES = 40 * 1024 * 1024


def halves(value):
    high = value.astype(BF16)
    return high, (value - high.astype(F32)).astype(BF16)


def stacked(value):
    return jnp.concatenate(halves(value), axis=0)


def folded(value):
    half = value.shape[0] // 2
    return value[:half] + value[half:]


def dot(first, second):
    return jnp.dot(first, second, preferred_element_type=F32)


def dot_last(first, second, precision=None):
    return lax.dot_general(
        first, second, (((1,), (1,)), ((), ())), preferred_element_type=F32, precision=precision
    )


def first_kernel(source_ref, send_ref, pick_ref, slab_ref, section_ref):
    owned = source_ref.shape[1]
    shared = send_ref.shape[1]
    faces = lax.broadcasted_iota(jnp.int32, (owned, shared), 0)
    for row in range(2):
        pick_ref[:, row * shared : (row + 1) * shared] = jnp.where(
            faces == send_ref[row : row + 1, :], 1.0, 0.0
        ).astype(BF16)
    sent = folded(dot(stacked(source_ref[...]), pick_ref[...]))
    slab_ref[...] = sent[:, :shared]
    section_ref[...] = sent[:, shared:]


def prepare_kernel(
    table_ref, inverse_ref, lifting_ref, block_ref, select_ref, weight_ref, scale_ref
):
    faces = select_ref.shape[0]
    elements = table_ref.shape[1]
    trace = block_ref.shape[1]
    shapes = block_ref.shape[0]
    dofs = trace // 4
    ids = lax.broadcasted_iota(jnp.int32, (faces, elements), 0)
    for k in range(4):
        select_ref[:, k * elements : (k + 1) * elements] = jnp.where(
            ids == table_ref[k : k + 1, :], 1.0, 0.0
        ).astype(BF16)
    place = lax.broadcasted_iota(jnp.int32, (trace, trace), 0)
    k = sum(jnp.where(place >= m * dofs, 1, 0) for m in range(1, 4))
    order = jnp.where(
        lax.broadcasted_iota(jnp.int32, (trace, trace), 1) == (place - k * dofs) * 4 + k, 1.0, 0.0
    )
    highest = lax.Precision.HIGHEST
    block_bound = jnp.zeros((1, 1), F32)
    inner_bound = jnp.zeros((1, 1), F32)
    for t in range(shapes):
        lifted = jnp.dot(order, lifting_ref[t], preferred_element_type=F32, precision=highest)
        inner = dot_last(dot_last(lifted, inverse_ref[t], highest), lifted, highest)
        block = dot_last(dot_last(order, block_ref[t], highest), order, highest)
        block_bound = jnp.maximum(block_bound, jnp.sum(block * block, keepdims=True))
        inner_bound = jnp.maximum(inner_bound, jnp.sum(inner * inner, keepdims=True))
        high, low = halves(jnp.concatenate([block, inner], axis=0))
        weight_ref[t] = jnp.concatenate([high, high, low], axis=1)
    bound = 4.0 * (6.0 + jnp.sqrt(block_bound) + 2.0 * jnp.sqrt(inner_bound)) + SHIFT
    scale_ref[...] = jnp.broadcast_to(
        jnp.maximum(1.0, bound * (1.0 / NORM_ROOM)), scale_ref.shape
    )


def inner_products(vectors, last, gram_ref, first_row):
    for i, vector in enumerate(vectors):
        gram_ref[first_row + i : first_row + i + 1, :] = lane_sums(vector * last)


def lane_sums(product):
    total = product[:, :128]
    for start in range(128, product.shape[1], 128):
        total = total + product[:, start : start + 128]
    return jnp.sum(total, axis=0, keepdims=True)


def apply_kernel(first, final, earlier, *refs):
    refs = list(refs)
    own_ref = refs.pop(0)
    ghosts = [refs.pop(0) for _ in range(2)]
    if not first:
        down = [refs.pop(0) for _ in range(2)]
        back = [refs.pop(0) for _ in range(2)]
    vectors = [refs.pop(0) for _ in range(earlier)]
    select_ref, weight_ref, pick_ref, stabilize_ref, coupling_ref, scale_ref = refs[:6]
    refs = refs[6:]
    if not first:
        vector_ref = refs.pop(0)
    gram_ref = refs.pop(0)
    part_ref = refs.pop(0)
    down_out = [refs.pop(0) for _ in range(2)]
    if not final:
        up_out = [refs.pop(0) for _ in range(2)]
    wide_ref, result_ref = refs

    dofs, owned = own_ref.shape
    shared = ghosts[0].shape[1]
    shapes = weight_ref.shape[0]
    elements = stabilize_ref.shape[1]
    group = elements // shapes
    trace = 4 * dofs

    if first:
        vector = own_ref[...]
        ghost = jnp.concatenate([ref[...] for ref in ghosts], axis=1)
    else:
        received = jnp.concatenate([ref[...] for ref in back], axis=1)
        vector = own_ref[...] + folded(dot_last(stacked(received), pick_ref[...]))
        vector_ref[...] = vector
        ghost = jnp.concatenate([a[...] + b[...] for a, b in zip(ghosts, down)], axis=1)
    extended = jnp.concatenate([vector, ghost], axis=1)
    wide_ref[...] = stacked(extended)

    for t in range(shapes):
        columns = slice(t * group, (t + 1) * group)
        picked = []
        for k in range(4):
            start = k * elements + t * group
            picked.append(dot(wide_ref[...], select_ref[:, start : start + group]))
        high = jnp.concatenate([p[:dofs] for p in picked], axis=0)
        low = jnp.concatenate([p[dofs:] for p in picked], axis=0)
        high16, low16 = high.astype(BF16), low.astype(BF16)
        product = dot(weight_ref[t], jnp.concatenate([high16, low16, high16], axis=0))
        result = (
            stabilize_ref[:, columns] * (high + low)
            + product[:trace]
            - product[trace:] / coupling_ref[:, columns]
        )
        for k in range(4):
            start = k * elements + t * group
            result_ref[:, start : start + group] = stacked(result[k * dofs : (k + 1) * dofs])
    inner_products([ref[...] for ref in vectors] + [vector], vector, gram_ref, 0)
    gram_ref[earlier + 1 :, :] = jnp.zeros((8 - earlier - 1, 128), F32)
    shrink = 1.0 / scale_ref[:, :1]
    summed = folded(dot_last(result_ref[...], select_ref[...])) * shrink
    part = summed[:, :owned] - (SHIFT * shrink) * vector
    part_ref[...] = part
    for i in range(2):
        down_out[i][...] = summed[:, owned + i * shared : owned + (i + 1) * shared]
    if not final:
        sent = folded(dot(stacked(part), pick_ref[...]))
        for i in range(2):
            up_out[i][...] = sent[:, i * shared : (i + 1) * shared]


def last_kernel(*refs):
    own_ref, slab_ref, section_ref = refs[:3]
    vectors = refs[3 : 3 + ITERS]
    grams = refs[3 + ITERS : 3 + 2 * ITERS]
    pick_ref, row_ref, sums_ref = refs[3 + 2 * ITERS :]
    received = jnp.concatenate([slab_ref[...], section_ref[...]], axis=1)
    vector = own_ref[...] + folded(dot_last(stacked(received), pick_ref[...]))
    sums_ref[...] = jnp.zeros(sums_ref.shape, F32)
    for j in range(ITERS):
        start = j * (j + 1) // 2
        sums_ref[start : start + j + 1, :] = grams[j][: j + 1, :]
    inner_products([ref[...] for ref in vectors] + [vector], vector, sums_ref, ITERS * (ITERS + 1) // 2)
    totals = jnp.sum(sums_ref[...], axis=1, keepdims=True)
    count = sums_ref.shape[0]
    diagonal = lax.broadcasted_iota(jnp.int32, (count, 128), 0) == lax.broadcasted_iota(
        jnp.int32, (count, 128), 1
    )
    row = jnp.sum(jnp.where(diagonal, totals, 0.0), axis=0, keepdims=True)
    row_ref[...] = jnp.broadcast_to(row, row_ref.shape)


def least_squares(hessenberg, target):
    breadth = len(hessenberg)
    height = len(target)
    unit_columns = []
    triangle = {}
    for k in range(breadth):
        column = list(hessenberg[k])
        for i in range(k):
            triangle[i, k] = sum(unit_columns[i][r] * column[r] for r in range(height))
            column = [column[r] - triangle[i, k] * unit_columns[i][r] for r in range(height)]
        triangle[k, k] = jnp.sqrt(sum(c * c for c in column))
        unit_columns.append([c / triangle[k, k] for c in column])
    projected = [sum(v[r] * target[r] for r in range(height)) for v in unit_columns]
    outcome = [None] * breadth
    for k in reversed(range(breadth)):
        running = projected[k]
        for i in range(k + 1, breadth):
            running = running - triangle[k, i] * outcome[i]
        outcome[k] = running / triangle[k, k]
    return outcome


def coefficients(gram, scale):
    size = ITERS + 1
    zero = jnp.zeros_like(scale)

    def inner(a, b):
        total = zero
        for i in range(size):
            for j in range(size):
                if a[i] is not None and b[j] is not None:
                    total = total + a[i] * b[j] * gram[i][j]
        return total

    def plus(a, factor, b):
        out = []
        for x, y in zip(a, b):
            if y is None:
                out.append(x)
            else:
                out.append(factor * y if x is None else x + factor * y)
        return out

    initial_norm = jnp.sqrt(gram[0][0] + EPSILON)
    krylov = [[1.0 / initial_norm] + [None] * ITERS]
    columns = []
    for j in range(ITERS):
        shifted = [None] + [scale * c if c is not None else None for c in krylov[j][:-1]]
        fresh = plus(shifted, SHIFT, krylov[j])
        products = [inner(vector, fresh) for vector in krylov]
        for value, vector in zip(products, krylov):
            fresh = plus(fresh, -value, vector)
        subdiag = jnp.sqrt(jnp.maximum(inner(fresh, fresh), 0.0) + EPSILON)
        columns.append(products + [subdiag] + [zero] * (ITERS - 1 - j))
        krylov.append([c / subdiag if c is not None else None for c in fresh])
    combine = least_squares(columns, [initial_norm] + [zero] * ITERS)
    total = [None] * size
    for y, vector in zip(combine, krylov):
        total = plus(total, y, vector)
    return total[:ITERS]


def solve_kernel(rows_ref, scale_ref, *refs):
    vectors = refs[:ITERS]
    out_ref = refs[ITERS]
    sums = jnp.sum(rows_ref[...], axis=0, keepdims=True)
    gram = [[None] * (ITERS + 1) for _ in range(ITERS + 1)]
    for p, (i, j) in enumerate(PAIRS):
        gram[i][j] = gram[j][i] = sums[:, p : p + 1]
    weights = coefficients(gram, scale_ref[:, :1])
    total = weights[0] * vectors[0][...]
    for weight, ref in zip(weights[1:], vectors[1:]):
        total = total + weight * ref[...]
    out_ref[...] = total


def passed_along(value, axis, steps):
    count = lax.axis_size(axis)
    pairs = [(source, (source + steps) % count) for source in range(count)]
    return lax.ppermute(value, axis, pairs)


def shape(*dims, dtype=F32):
    return jax.ShapeDtypeStruct(dims, dtype)


def call(kernel, out_shape, *args, scratch=(), flops=0, name=None):
    return pl.pallas_call(
        kernel,
        out_shape=out_shape,
        in_specs=[pl.BlockSpec(memory_space=pltpu.VMEM)] * len(args),
        out_specs=jax.tree.map(lambda _: pl.BlockSpec(memory_space=pltpu.VMEM), out_shape),
        scratch_shapes=list(scratch),
        cost_estimate=pl.CostEstimate(flops=flops, bytes_accessed=4 * 1024 * 1024, transcendentals=0),
        compiler_params=pltpu.CompilerParams(vmem_limit_bytes=VMEM_BYTES),
        name=name,
    )(*args)


def per_device(
    right_side, face_table, send_faces, stabilize, coupling, inverse, lifting, trace_block
):
    source = right_side[0, 0]
    table = face_table[0, 0]
    send_lists = send_faces[0, 0]
    penalty = stabilize[0]
    scaling = coupling[0]
    dofs, owned = source.shape
    elements = table.shape[1]
    shared = send_lists.shape[1]
    faces = owned + 2 * shared
    shapes, trace, _ = lifting.shape
    devices = lax.axis_size("gx") * lax.axis_size("yz")
    part = shape(dofs, shared)

    pick, slab, section = call(
        first_kernel, (shape(owned, 2 * shared, dtype=BF16), part, part), source, send_lists, name="first"
    )
    ghosts = [passed_along(slab, "gx", 1), passed_along(section, "yz", 1)]
    select, weights, scale = call(
        prepare_kernel,
        (
            shape(faces, 4 * elements, dtype=BF16),
            shape(shapes, 2 * trace, 3 * trace, dtype=BF16),
            shape(1, 128),
        ),
        table,
        inverse,
        lifting,
        trace_block,
        flops=2 * 10**9,
        name="prepare",
    )
    vectors = [source]
    grams = []
    own, exchanged = source, ghosts
    for j in range(ITERS):
        final = j == ITERS - 1
        outs = [shape(8, 128), shape(dofs, owned), part, part]
        if j:
            outs = [shape(dofs, owned)] + outs
        if not final:
            outs = outs + [part, part]
        earlier = vectors[:j] if j else []
        results = call(
            functools.partial(apply_kernel, j == 0, final, len(earlier)),
            tuple(outs),
            own,
            *exchanged,
            *earlier,
            select,
            weights,
            pick,
            penalty,
            scaling,
            scale,
            scratch=[pltpu.VMEM((2 * dofs, faces), BF16), pltpu.VMEM((2 * dofs, 4 * elements), BF16)],
            flops=2 * 10**9,
            name=f"apply{j}",
        )
        results = list(results)
        if j:
            vectors.append(results.pop(0))
        grams.append(results.pop(0))
        own = results.pop(0)
        down = [results.pop(0) for _ in range(2)]
        back = [passed_along(down[0], "gx", -1), passed_along(down[1], "yz", -1)]
        if final:
            exchanged = back
        else:
            up = [passed_along(results.pop(0), "gx", 1), passed_along(results.pop(0), "yz", 1)]
            exchanged = up + down + back
    rows = call(
        last_kernel, shape(devices, 128), own, *exchanged, *vectors, *grams, pick, scratch=[pltpu.VMEM((16, 128), F32)],
        name="last",
    )
    rows = lax.all_to_all(rows.reshape(devices, 1, 128), ("gx", "yz"), 0, 0).reshape(devices, 128)
    solution = call(solve_kernel, shape(dofs, owned), rows, scale, *vectors, name="solve")
    return solution[None, None]


def solution(mesh):
    return jax.shard_map(
        per_device,
        mesh=mesh,
        in_specs=(
            P("gx", "yz", None, None),
            P("gx", "yz", None, None),
            P("gx", "yz", None, None),
            P("gx", "yz", None),
            P("gx", "yz", None),
            P(),
            P(),
            P(),
        ),
        out_specs=P("gx", "yz", None, None),
        check_vma=False,
    )
```

```python
import functools

import jax
import jax.numpy as jnp
from jax import lax
from jax.experimental import pallas as pl
from jax.experimental.pallas import tpu as pltpu
from jax.sharding import PartitionSpec as P

ITERS = 4
EPSILON = 1e-06
SHIFT = 12.0
NORM_ROOM = 1024.0
F32 = jnp.float32
BF16 = jnp.bfloat16
STARTS = ("gx later", "gx first", "yz up", "yz down")
PAIRS = [(i, j) for j in range(ITERS + 1) for i in range(j + 1)]
VMEM_BYTES = 20 * 1024 * 1024


def halves(value):
    high = value.astype(BF16)
    return high, (value - high.astype(F32)).astype(BF16)


def stacked(value):
    return jnp.concatenate(halves(value), axis=0)


def folded(value):
    half = value.shape[0] // 2
    return value[:half] + value[half:]


def dot(first, second):
    return jnp.dot(first, second, preferred_element_type=F32)


def dot_last(first, second, precision=None):
    return lax.dot_general(
        first, second, (((1,), (1,)), ((), ())), preferred_element_type=F32, precision=precision
    )


def fetched(sources, targets, semaphores):
    copies = [
        pltpu.make_async_copy(source, target, semaphores.at[k])
        for k, (source, target) in enumerate(zip(sources, targets))
    ]
    for copy in copies:
        copy.start()
    return [copy.wait for copy in copies]


def first_kernel(source_hbm, send_hbm, pick_ref, slab_ref, section_ref, source_ref, send_ref, semaphores):
    have_source, have_send = fetched((source_hbm, send_hbm), (source_ref, send_ref), semaphores)
    owned = source_ref.shape[1]
    shared = send_ref.shape[1]
    faces = lax.broadcasted_iota(jnp.int32, (owned, shared), 0)
    have_send()
    for row in range(2):
        pick_ref[:, row * shared : (row + 1) * shared] = jnp.where(
            faces == send_ref[row : row + 1, :], 1.0, 0.0
        ).astype(BF16)
    have_source()
    sent = folded(dot(stacked(source_ref[...]), pick_ref[...]))
    slab_ref[...] = sent[:, :shared]
    section_ref[...] = sent[:, shared:]


def three_pass(first, second):
    return dot_last(first[0], second[0]) + (dot_last(first[0], second[1]) + dot_last(first[1], second[0]))


def prepare_kernel(
    table_hbm, inverse_hbm, lifting_hbm, block_hbm, select_ref, weight_ref, scale_ref,
    table_ref, inverse_ref, lifting_ref, block_ref, semaphores,
):
    have_table, have_inverse, have_lifting, have_block = fetched(
        (table_hbm, inverse_hbm, lifting_hbm, block_hbm),
        (table_ref, inverse_ref, lifting_ref, block_ref),
        semaphores,
    )
    faces = select_ref.shape[0]
    elements = table_ref.shape[1]
    trace = block_ref.shape[1]
    shapes = block_ref.shape[0]
    dofs = trace // 4
    place = lax.broadcasted_iota(jnp.int32, (trace, trace), 0)
    k = sum(jnp.where(place >= m * dofs, 1, 0) for m in range(1, 4))
    order = jnp.where(
        lax.broadcasted_iota(jnp.int32, (trace, trace), 1) == (place - k * dofs) * 4 + k, 1.0, 0.0
    ).astype(BF16)
    have_table()
    group = elements // shapes
    ids = lax.broadcasted_iota(jnp.int32, (faces, group), 0)
    for t in range(shapes):
        for k in range(4):
            start = (t * 4 + k) * group
            select_ref[:, start : start + group] = jnp.where(
                ids == table_ref[k : k + 1, t * group : (t + 1) * group], 1.0, 0.0
            ).astype(BF16)
    block_bound = jnp.zeros((1, 1), F32)
    inner_bound = jnp.zeros((1, 1), F32)
    have_inverse()
    have_lifting()
    have_block()
    for t in range(shapes):
        lifted = [dot_last(order, part).astype(BF16) for part in halves(lifting_ref[t])]
        half = three_pass(lifted, halves(inverse_ref[t]))
        inner = three_pass(halves(half), lifted)
        turned = [dot_last(order, part).astype(BF16) for part in halves(block_ref[t])]
        block = [dot_last(part, order) for part in turned]
        square = block[0] + block[1]
        block_bound = jnp.maximum(block_bound, jnp.sum(square * square, keepdims=True))
        inner_bound = jnp.maximum(inner_bound, jnp.sum(inner * inner, keepdims=True))
        inner_high, inner_low = halves(inner)
        high = jnp.concatenate([block[0].astype(BF16), inner_high], axis=0)
        low = jnp.concatenate([block[1].astype(BF16), inner_low], axis=0)
        weight_ref[t] = jnp.concatenate([high, high, low], axis=1)
    bound = 4.0 * (6.0 + jnp.sqrt(block_bound) + 2.0 * jnp.sqrt(inner_bound)) + SHIFT
    scale_ref[...] = jnp.broadcast_to(
        jnp.maximum(1.0, bound * (1.0 / NORM_ROOM)), scale_ref.shape
    )


def inner_products(vectors, last, gram_ref, first_row):
    for i, vector in enumerate(vectors):
        gram_ref[first_row + i : first_row + i + 1, :] = lane_sums(vector * last)


def lane_sums(product):
    total = product[:, :128]
    for start in range(128, product.shape[1], 128):
        total = total + product[:, start : start + 128]
    return jnp.sum(total, axis=0, keepdims=True)


def apply_kernel(first, final, earlier, *refs):
    refs = list(refs)
    own_ref = refs.pop(0)
    if first:
        ghosts = [refs.pop(0) for _ in range(2)]
    else:
        got = [refs.pop(0) for _ in range(4)]
        down = [refs.pop(0) for _ in range(2)]
    vectors = [refs.pop(0) for _ in range(earlier)]
    select_ref, weight_ref, pick_ref, stabilize_ref, coupling_ref, scale_ref, odd_ref = refs[:7]
    refs = refs[7:]
    if not first:
        vector_ref = refs.pop(0)
    gram_ref = refs.pop(0)
    part_ref = refs.pop(0)
    down_out = [refs.pop(0) for _ in range(2)]
    if not final:
        message = [refs.pop(0) for _ in range(4)]
    (wide_ref,) = refs
    odd = odd_ref[...] != 0

    dofs, owned = own_ref.shape
    shared = pick_ref.shape[1] // 2
    shapes = weight_ref.shape[0]
    elements = stabilize_ref.shape[1]
    group = elements // shapes
    trace = 4 * dofs

    if first:
        vector = own_ref[...]
        ghost = jnp.concatenate([ref[...] for ref in ghosts], axis=1)
    else:
        parts = dict(zip(STARTS, [ref[...] for ref in got]))
        back = [jnp.where(odd, parts["gx later"], parts["gx first"]), parts["yz down"]]
        up = [jnp.where(odd, parts["gx first"], parts["gx later"]), parts["yz up"]]
        received = jnp.concatenate(back, axis=1)
        vector = own_ref[...] + folded(dot_last(stacked(received), pick_ref[...]))
        vector_ref[...] = vector
        ghost = jnp.concatenate([a + b[...] for a, b in zip(up, down)], axis=1)
    extended = jnp.concatenate([vector, ghost], axis=1)
    wide_ref[...] = stacked(extended)

    everything = dot(wide_ref[...], select_ref[...])
    results = []
    for t in range(shapes):
        columns = slice(t * group, (t + 1) * group)
        picked = [everything[:, (t * 4 + k) * group : (t * 4 + k + 1) * group] for k in range(4)]
        high = jnp.concatenate([p[:dofs] for p in picked], axis=0)
        low = jnp.concatenate([p[dofs:] for p in picked], axis=0)
        high16, low16 = high.astype(BF16), low.astype(BF16)
        product = dot(weight_ref[t], jnp.concatenate([high16, low16, high16], axis=0))
        result = (
            stabilize_ref[:, columns] * (high + low)
            + product[:trace]
            - product[trace:] / coupling_ref[:, columns]
        )
        results += [stacked(result[k * dofs : (k + 1) * dofs]) for k in range(4)]
    inner_products([ref[...] for ref in vectors] + [vector], vector, gram_ref, 0)
    gram_ref[earlier + 1 :, :] = jnp.zeros((8 - earlier - 1, 128), F32)
    shrink = 1.0 / scale_ref[:, :1]
    summed = folded(dot_last(jnp.concatenate(results, axis=1), select_ref[...])) * shrink
    part = summed[:, :owned] - (SHIFT * shrink) * vector
    part_ref[...] = part
    for i in range(2):
        down_out[i][...] = summed[:, owned + i * shared : owned + (i + 1) * shared]
    if not final:
        sent = folded(dot(stacked(part), pick_ref[...]))
        up, up_section = sent[:, :shared], sent[:, shared:]
        down, down_section = summed[:, owned : owned + shared], summed[:, owned + shared :]
        parts = {
            "gx later": jnp.where(odd, up, down),
            "gx first": jnp.where(odd, down, up),
            "yz up": up_section,
            "yz down": down_section,
        }
        for name, ref in zip(STARTS, message):
            ref[...] = parts[name]


def last_kernel(*refs):
    own_ref, slab_ref, section_ref = refs[:3]
    vectors = refs[3 : 3 + ITERS]
    grams = refs[3 + ITERS : 3 + 2 * ITERS]
    pick_ref, row_ref, sums_ref = refs[3 + 2 * ITERS :]
    received = jnp.concatenate([slab_ref[...], section_ref[...]], axis=1)
    vector = own_ref[...] + folded(dot_last(stacked(received), pick_ref[...]))
    sums_ref[...] = jnp.zeros(sums_ref.shape, F32)
    for j in range(ITERS):
        start = j * (j + 1) // 2
        sums_ref[start : start + j + 1, :] = grams[j][: j + 1, :]
    inner_products([ref[...] for ref in vectors] + [vector], vector, sums_ref, ITERS * (ITERS + 1) // 2)
    totals = jnp.sum(sums_ref[...], axis=1, keepdims=True)
    count = sums_ref.shape[0]
    diagonal = lax.broadcasted_iota(jnp.int32, (count, 128), 0) == lax.broadcasted_iota(
        jnp.int32, (count, 128), 1
    )
    row = jnp.sum(jnp.where(diagonal, totals, 0.0), axis=0, keepdims=True)
    row_ref[...] = jnp.broadcast_to(row, row_ref.shape)


def least_squares(hessenberg, target):
    breadth = len(hessenberg)
    height = len(target)
    unit_columns = []
    triangle = {}
    for k in range(breadth):
        column = list(hessenberg[k])
        for i in range(k):
            triangle[i, k] = sum(unit_columns[i][r] * column[r] for r in range(height))
            column = [column[r] - triangle[i, k] * unit_columns[i][r] for r in range(height)]
        triangle[k, k] = jnp.sqrt(sum(c * c for c in column))
        unit_columns.append([c / triangle[k, k] for c in column])
    projected = [sum(v[r] * target[r] for r in range(height)) for v in unit_columns]
    outcome = [None] * breadth
    for k in reversed(range(breadth)):
        running = projected[k]
        for i in range(k + 1, breadth):
            running = running - triangle[k, i] * outcome[i]
        outcome[k] = running / triangle[k, k]
    return outcome


def coefficients(gram, scale):
    size = ITERS + 1
    zero = jnp.zeros_like(scale)

    def inner(a, b):
        total = zero
        for i in range(size):
            for j in range(size):
                if a[i] is not None and b[j] is not None:
                    total = total + a[i] * b[j] * gram[i][j]
        return total

    def plus(a, factor, b):
        out = []
        for x, y in zip(a, b):
            if y is None:
                out.append(x)
            else:
                out.append(factor * y if x is None else x + factor * y)
        return out

    initial_norm = jnp.sqrt(gram[0][0] + EPSILON)
    krylov = [[1.0 / initial_norm] + [None] * ITERS]
    columns = []
    for j in range(ITERS):
        shifted = [None] + [scale * c if c is not None else None for c in krylov[j][:-1]]
        fresh = plus(shifted, SHIFT, krylov[j])
        products = [inner(vector, fresh) for vector in krylov]
        for value, vector in zip(products, krylov):
            fresh = plus(fresh, -value, vector)
        subdiag = jnp.sqrt(jnp.maximum(inner(fresh, fresh), 0.0) + EPSILON)
        columns.append(products + [subdiag] + [zero] * (ITERS - 1 - j))
        krylov.append([c / subdiag if c is not None else None for c in fresh])
    combine = least_squares(columns, [initial_norm] + [zero] * ITERS)
    total = [None] * size
    for y, vector in zip(combine, krylov):
        total = plus(total, y, vector)
    return total[:ITERS]


def add_kernel(rows_ref, out_ref):
    total = jnp.sum(rows_ref[...], axis=0, keepdims=True)
    out_ref[...] = jnp.broadcast_to(total, out_ref.shape)


def solve_kernel(rows_ref, scale_ref, *refs):
    vectors = refs[:ITERS]
    out_ref = refs[ITERS]
    sums = jnp.sum(rows_ref[...], axis=0, keepdims=True)
    gram = [[None] * (ITERS + 1) for _ in range(ITERS + 1)]
    for p, (i, j) in enumerate(PAIRS):
        gram[i][j] = gram[j][i] = sums[:, p : p + 1]
    weights = coefficients(gram, scale_ref[:, :1])
    total = weights[0] * vectors[0][...]
    for weight, ref in zip(weights[1:], vectors[1:]):
        total = total + weight * ref[...]
    out_ref[...] = total


def passed_along(value, axis, steps):
    count = lax.axis_size(axis)
    pairs = [(source, (source + steps) % count) for source in range(count)]
    return lax.ppermute(value, axis, pairs)


def exchange(value, name):
    axis, kind = name.split()
    if kind in ("up", "down"):
        return passed_along(value, axis, 1 if kind == "up" else -1)
    count = lax.axis_size(axis)
    ahead = 1 if kind == "later" else 0
    pairs = [(i, (i + (1 if i % 2 == ahead else -1)) % count) for i in range(count)]
    return lax.ppermute(value, axis, pairs)


def every(row, axis):
    count = row.shape[0]
    return lax.all_to_all(row.reshape(count, 1, 128), axis, 0, 0).reshape(count, 128)


def shape(*dims, dtype=F32):
    return jax.ShapeDtypeStruct(dims, dtype)


def call(kernel, out_shape, *args, scratch=(), flops=0, name=None, space=pltpu.VMEM):
    if space == pltpu.HBM:
        args = [pltpu.with_memory_space_constraint(arg, space) for arg in args]
    return pl.pallas_call(
        kernel,
        out_shape=out_shape,
        in_specs=[pl.BlockSpec(memory_space=space)] * len(args),
        out_specs=jax.tree.map(lambda _: pl.BlockSpec(memory_space=pltpu.VMEM), out_shape),
        scratch_shapes=list(scratch),
        cost_estimate=pl.CostEstimate(flops=flops, bytes_accessed=4 * 1024 * 1024, transcendentals=0),
        compiler_params=pltpu.CompilerParams(vmem_limit_bytes=VMEM_BYTES),
        name=name,
    )(*args)


def per_device(
    right_side, face_table, send_faces, stabilize, coupling, inverse, lifting, trace_block
):
    source = right_side[0, 0]
    table = face_table[0, 0]
    send_lists = send_faces[0, 0]
    penalty = stabilize[0]
    scaling = coupling[0]
    dofs, owned = source.shape
    elements = table.shape[1]
    shared = send_lists.shape[1]
    faces = owned + 2 * shared
    shapes, trace, _ = lifting.shape
    part = shape(dofs, shared)

    pick, slab, section = call(
        first_kernel,
        (shape(owned, 2 * shared, dtype=BF16), part, part),
        source,
        send_lists,
        scratch=[
            pltpu.VMEM(source.shape, F32),
            pltpu.VMEM(send_lists.shape, jnp.int32),
            pltpu.SemaphoreType.DMA((2,)),
        ],
        name="first",
        space=pltpu.HBM,
    )
    ghosts = [passed_along(slab, "gx", 1), passed_along(section, "yz", 1)]
    turned = jnp.swapaxes(lifting, 1, 2)
    select, weights, scale = call(
        prepare_kernel,
        (
            shape(faces, 4 * elements, dtype=BF16),
            shape(shapes, 2 * trace, 3 * trace, dtype=BF16),
            shape(1, 128),
        ),
        table,
        inverse,
        turned,
        trace_block,
        scratch=[
            pltpu.VMEM(table.shape, jnp.int32),
            pltpu.VMEM(inverse.shape, F32),
            pltpu.VMEM(turned.shape, F32),
            pltpu.VMEM(trace_block.shape, F32),
            pltpu.SemaphoreType.DMA((4,)),
        ],
        flops=2 * 10**9,
        name="prepare",
        space=pltpu.HBM,
    )
    odd = jnp.full((1, 128), lax.axis_index("gx") % 2, jnp.int32)
    vectors = [source]
    grams = []
    own, exchanged = source, ghosts
    for j in range(ITERS):
        final = j == ITERS - 1
        outs = [shape(8, 128), shape(dofs, owned), part, part]
        if j:
            outs = [shape(dofs, owned)] + outs
        if not final:
            outs = outs + [part] * 4
        earlier = vectors[:j] if j else []
        results = call(
            functools.partial(apply_kernel, j == 0, final, len(earlier)),
            tuple(outs),
            own,
            *exchanged,
            *earlier,
            select,
            weights,
            pick,
            penalty,
            scaling,
            scale,
            odd,
            scratch=[pltpu.VMEM((2 * dofs, faces), BF16)],
            flops=2 * 10**9,
            name=f"apply{j}",
        )
        results = list(results)
        if j:
            vectors.append(results.pop(0))
        grams.append(results.pop(0))
        own = results.pop(0)
        down = [results.pop(0) for _ in range(2)]
        if final:
            exchanged = [passed_along(down[0], "gx", -1), passed_along(down[1], "yz", -1)]
        else:
            exchanged = [exchange(results.pop(0), name) for name in STARTS] + down
    gx, yz = lax.axis_size("gx"), lax.axis_size("yz")
    rows = call(
        last_kernel,
        shape(yz, 128),
        own,
        *exchanged,
        *vectors,
        *grams,
        pick,
        scratch=[pltpu.VMEM((16, 128), F32)],
        name="last",
    )
    rows = call(add_kernel, shape(gx, 128), every(rows, "yz"), name="add")
    solution = call(solve_kernel, shape(dofs, owned), every(rows, "gx"), scale, *vectors, name="solve")
    return solution[None, None]


def solution(mesh):
    return jax.shard_map(
        per_device,
        mesh=mesh,
        in_specs=(
            P("gx", "yz", None, None),
            P("gx", "yz", None, None),
            P("gx", "yz", None, None),
            P("gx", "yz", None),
            P("gx", "yz", None),
            P(),
            P(),
            P(),
        ),
        out_specs=P("gx", "yz", None, None),
        check_vma=False,
    )
```

```python
import functools

import jax
import jax.numpy as jnp
from jax import lax
from jax.experimental import pallas as pl
from jax.experimental.pallas import tpu as pltpu
from jax.sharding import PartitionSpec as P

ITERS = 4
EPSILON = 1e-06
SHIFT = 12.0
NORM_ROOM = 1024.0
F32 = jnp.float32
BF16 = jnp.bfloat16
STARTS = ("gx later", "gx first", "yz up", "yz down")
PAIRS = [(i, j) for j in range(ITERS + 1) for i in range(j + 1)]
VMEM_BYTES = 20 * 1024 * 1024


def halves(value):
    high = value.astype(BF16)
    return high, (value - high.astype(F32)).astype(BF16)


def stacked(value):
    return jnp.concatenate(halves(value), axis=0)


def folded(value):
    half = value.shape[0] // 2
    return value[:half] + value[half:]


def dot(first, second):
    return jnp.dot(first, second, preferred_element_type=F32)


def dot_last(first, second, precision=None):
    return lax.dot_general(
        first, second, (((1,), (1,)), ((), ())), preferred_element_type=F32, precision=precision
    )


def fetched(sources, targets, semaphores):
    copies = [
        pltpu.make_async_copy(source, target, semaphores.at[k])
        for k, (source, target) in enumerate(zip(sources, targets))
    ]
    for copy in copies:
        copy.start()
    return [copy.wait for copy in copies]


def first_kernel(source_hbm, send_hbm, pick_ref, slab_ref, section_ref, source_ref, send_ref, semaphores):
    have_source, have_send = fetched((source_hbm, send_hbm), (source_ref, send_ref), semaphores)
    owned = source_ref.shape[1]
    shared = send_ref.shape[1]
    faces = lax.broadcasted_iota(jnp.int32, (owned, shared), 0)
    have_send()
    for row in range(2):
        pick_ref[:, row * shared : (row + 1) * shared] = jnp.where(
            faces == send_ref[row : row + 1, :], 1.0, 0.0
        ).astype(BF16)
    have_source()
    sent = folded(dot(stacked(source_ref[...]), pick_ref[...]))
    slab_ref[...] = sent[:, :shared]
    section_ref[...] = sent[:, shared:]


def three_pass(first, second):
    return dot_last(first[0], second[0]) + (dot_last(first[0], second[1]) + dot_last(first[1], second[0]))


def by_face(value, rows_ref, slot):
    rows, columns = value.shape
    parts = []
    for start in range(0, columns, 128):
        width = min(128, columns - start)
        rows_ref[slot, :, :width] = value[:, start : start + width]
        part = jnp.concatenate([rows_ref[slot, pl.ds(k, rows // 4, stride=4), :] for k in range(4)], axis=0)
        parts.append(part[:, :width])
        slot += 1
    return jnp.concatenate(parts, axis=1)


def prepare_kernel(
    table_hbm, inverse_hbm, lifting_hbm, block_hbm, select_ref, weight_ref, scale_ref,
    table_ref, inverse_ref, lifting_ref, block_ref, rows_ref, semaphores,
):
    have_table, have_inverse, have_lifting, have_block = fetched(
        (table_hbm, inverse_hbm, lifting_hbm, block_hbm),
        (table_ref, inverse_ref, lifting_ref, block_ref),
        semaphores,
    )
    faces = select_ref.shape[0]
    elements = table_ref.shape[1]
    shapes = block_ref.shape[0]
    have_table()
    group = elements // shapes
    ids = lax.broadcasted_iota(jnp.int32, (faces, group), 0)
    for t in range(shapes):
        for k in range(4):
            start = (t * 4 + k) * group
            select_ref[:, start : start + group] = jnp.where(
                ids == table_ref[k : k + 1, t * group : (t + 1) * group], 1.0, 0.0
            ).astype(BF16)
    block_bound = jnp.zeros((1, 1), F32)
    inner_bound = jnp.zeros((1, 1), F32)
    have_inverse()
    have_lifting()
    have_block()
    for t in range(shapes):
        lifted = halves(by_face(lifting_ref[t].T, rows_ref, 8 * t))
        inner = three_pass(halves(three_pass(lifted, halves(inverse_ref[t]))), lifted)
        block = by_face(by_face(block_ref[t], rows_ref, 8 * t + 2).T, rows_ref, 8 * t + 5)
        block_bound = jnp.maximum(block_bound, jnp.sum(block * block, keepdims=True))
        inner_bound = jnp.maximum(inner_bound, jnp.sum(inner * inner, keepdims=True))
        high, low = halves(jnp.concatenate([block, inner], axis=0))
        weight_ref[t] = jnp.concatenate([high, high, low], axis=1)
    bound = 4.0 * (6.0 + jnp.sqrt(block_bound) + 2.0 * jnp.sqrt(inner_bound)) + SHIFT
    scale_ref[...] = jnp.broadcast_to(
        jnp.maximum(1.0, bound * (1.0 / NORM_ROOM)), scale_ref.shape
    )


def inner_products(vectors, last, gram_ref, first_row):
    for i, vector in enumerate(vectors):
        gram_ref[first_row + i : first_row + i + 1, :] = lane_sums(vector * last)


def lane_sums(product):
    total = product[:, :128]
    for start in range(128, product.shape[1], 128):
        total = total + product[:, start : start + 128]
    return jnp.sum(total, axis=0, keepdims=True)


def apply_kernel(first, final, earlier, *refs):
    refs = list(refs)
    own_ref = refs.pop(0)
    if first:
        ghosts = [refs.pop(0) for _ in range(2)]
    else:
        got = [refs.pop(0) for _ in range(4)]
        down = [refs.pop(0) for _ in range(2)]
    vectors = [refs.pop(0) for _ in range(earlier)]
    select_ref, weight_ref, pick_ref, stabilize_ref, coupling_ref, scale_ref, odd_ref = refs[:7]
    refs = refs[7:]
    if not first:
        vector_ref = refs.pop(0)
    gram_ref = refs.pop(0)
    part_ref = refs.pop(0)
    down_out = [refs.pop(0) for _ in range(2)]
    if not final:
        message = [refs.pop(0) for _ in range(4)]
    (wide_ref,) = refs
    odd = odd_ref[:1, :] != 0

    dofs, owned = own_ref.shape
    shared = pick_ref.shape[1] // 2
    shapes = weight_ref.shape[0]
    elements = stabilize_ref.shape[1]
    group = elements // shapes
    trace = 4 * dofs

    if first:
        vector = own_ref[...]
        ghost = jnp.concatenate([ref[...] for ref in ghosts], axis=1)
    else:
        parts = dict(zip(STARTS, [ref[...] for ref in got]))
        back = [jnp.where(odd, parts["gx later"], parts["gx first"]), parts["yz down"]]
        up = [jnp.where(odd, parts["gx first"], parts["gx later"]), parts["yz up"]]
        received = jnp.concatenate(back, axis=1)
        vector = own_ref[...] + folded(dot_last(stacked(received), pick_ref[...]))
        vector_ref[...] = vector
        ghost = jnp.concatenate([a + b[...] for a, b in zip(up, down)], axis=1)
    extended = jnp.concatenate([vector, ghost], axis=1)
    wide_ref[...] = stacked(extended)

    everything = dot(wide_ref[...], select_ref[...])
    results = []
    for t in range(shapes):
        columns = slice(t * group, (t + 1) * group)
        picked = [everything[:, (t * 4 + k) * group : (t * 4 + k + 1) * group] for k in range(4)]
        high = jnp.concatenate([p[:dofs] for p in picked], axis=0)
        low = jnp.concatenate([p[dofs:] for p in picked], axis=0)
        high16, low16 = high.astype(BF16), low.astype(BF16)
        product = dot(weight_ref[t], jnp.concatenate([high16, low16, high16], axis=0))
        result = (
            stabilize_ref[:, columns] * (high + low)
            + product[:trace]
            - product[trace:] / coupling_ref[:, columns]
        )
        results += [stacked(result[k * dofs : (k + 1) * dofs]) for k in range(4)]
    inner_products([ref[...] for ref in vectors] + [vector], vector, gram_ref, 0)
    gram_ref[earlier + 1 :, :] = jnp.zeros((8 - earlier - 1, 128), F32)
    shrink = 1.0 / scale_ref[:, :1]
    summed = folded(dot_last(jnp.concatenate(results, axis=1), select_ref[...])) * shrink
    part = summed[:, :owned] - (SHIFT * shrink) * vector
    part_ref[...] = part
    for i in range(2):
        down_out[i][...] = summed[:, owned + i * shared : owned + (i + 1) * shared]
    if not final:
        sent = folded(dot(stacked(part), pick_ref[...]))
        up, up_section = sent[:, :shared], sent[:, shared:]
        down, down_section = summed[:, owned : owned + shared], summed[:, owned + shared :]
        parts = {
            "gx later": jnp.where(odd, up, down),
            "gx first": jnp.where(odd, down, up),
            "yz up": up_section,
            "yz down": down_section,
        }
        for name, ref in zip(STARTS, message):
            ref[...] = parts[name]


def last_kernel(*refs):
    own_ref, slab_ref, section_ref = refs[:3]
    vectors = refs[3 : 3 + ITERS]
    grams = refs[3 + ITERS : 3 + 2 * ITERS]
    pick_ref, row_ref, sums_ref = refs[3 + 2 * ITERS :]
    received = jnp.concatenate([slab_ref[...], section_ref[...]], axis=1)
    vector = own_ref[...] + folded(dot_last(stacked(received), pick_ref[...]))
    sums_ref[...] = jnp.zeros(sums_ref.shape, F32)
    for j in range(ITERS):
        start = j * (j + 1) // 2
        sums_ref[start : start + j + 1, :] = grams[j][: j + 1, :]
    inner_products([ref[...] for ref in vectors] + [vector], vector, sums_ref, ITERS * (ITERS + 1) // 2)
    totals = jnp.sum(sums_ref[...], axis=1, keepdims=True)
    count = sums_ref.shape[0]
    diagonal = lax.broadcasted_iota(jnp.int32, (count, 128), 0) == lax.broadcasted_iota(
        jnp.int32, (count, 128), 1
    )
    row = jnp.sum(jnp.where(diagonal, totals, 0.0), axis=0, keepdims=True)
    row_ref[...] = jnp.broadcast_to(row, row_ref.shape)


def least_squares(hessenberg, target):
    breadth = len(hessenberg)
    height = len(target)
    unit_columns = []
    triangle = {}
    for k in range(breadth):
        column = list(hessenberg[k])
        for i in range(k):
            triangle[i, k] = sum(unit_columns[i][r] * column[r] for r in range(height))
            column = [column[r] - triangle[i, k] * unit_columns[i][r] for r in range(height)]
        triangle[k, k] = jnp.sqrt(sum(c * c for c in column))
        unit_columns.append([c / triangle[k, k] for c in column])
    projected = [sum(v[r] * target[r] for r in range(height)) for v in unit_columns]
    outcome = [None] * breadth
    for k in reversed(range(breadth)):
        running = projected[k]
        for i in range(k + 1, breadth):
            running = running - triangle[k, i] * outcome[i]
        outcome[k] = running / triangle[k, k]
    return outcome


def coefficients(gram, scale):
    size = ITERS + 1
    zero = jnp.zeros_like(scale)

    def inner(a, b):
        total = zero
        for i in range(size):
            for j in range(size):
                if a[i] is not None and b[j] is not None:
                    total = total + a[i] * b[j] * gram[i][j]
        return total

    def plus(a, factor, b):
        out = []
        for x, y in zip(a, b):
            if y is None:
                out.append(x)
            else:
                out.append(factor * y if x is None else x + factor * y)
        return out

    initial_norm = jnp.sqrt(gram[0][0] + EPSILON)
    krylov = [[1.0 / initial_norm] + [None] * ITERS]
    columns = []
    for j in range(ITERS):
        shifted = [None] + [scale * c if c is not None else None for c in krylov[j][:-1]]
        fresh = plus(shifted, SHIFT, krylov[j])
        products = [inner(vector, fresh) for vector in krylov]
        for value, vector in zip(products, krylov):
            fresh = plus(fresh, -value, vector)
        subdiag = jnp.sqrt(jnp.maximum(inner(fresh, fresh), 0.0) + EPSILON)
        columns.append(products + [subdiag] + [zero] * (ITERS - 1 - j))
        krylov.append([c / subdiag if c is not None else None for c in fresh])
    combine = least_squares(columns, [initial_norm] + [zero] * ITERS)
    total = [None] * size
    for y, vector in zip(combine, krylov):
        total = plus(total, y, vector)
    return total[:ITERS]


def add_kernel(rows_ref, out_ref):
    total = jnp.sum(rows_ref[...], axis=0, keepdims=True)
    out_ref[...] = jnp.broadcast_to(total, out_ref.shape)


def solve_kernel(rows_ref, scale_ref, *refs):
    vectors = refs[:ITERS]
    out_ref = refs[ITERS]
    sums = jnp.sum(rows_ref[...], axis=0, keepdims=True)
    gram = [[None] * (ITERS + 1) for _ in range(ITERS + 1)]
    for p, (i, j) in enumerate(PAIRS):
        gram[i][j] = gram[j][i] = sums[:, p : p + 1]
    weights = coefficients(gram, scale_ref[:, :1])
    total = weights[0] * vectors[0][...]
    for weight, ref in zip(weights[1:], vectors[1:]):
        total = total + weight * ref[...]
    out_ref[...] = total


def passed_along(value, axis, steps):
    count = lax.axis_size(axis)
    pairs = [(source, (source + steps) % count) for source in range(count)]
    return lax.ppermute(value, axis, pairs)


def exchange(value, name):
    axis, kind = name.split()
    if kind in ("up", "down"):
        return passed_along(value, axis, 1 if kind == "up" else -1)
    count = lax.axis_size(axis)
    ahead = 1 if kind == "later" else 0
    pairs = [(i, (i + (1 if i % 2 == ahead else -1)) % count) for i in range(count)]
    return lax.ppermute(value, axis, pairs)


def every(row, axis):
    count = row.shape[0]
    return lax.all_to_all(row.reshape(count, 1, 128), axis, 0, 0).reshape(count, 128)


def shape(*dims, dtype=F32):
    return jax.ShapeDtypeStruct(dims, dtype)


def call(kernel, out_shape, *args, scratch=(), flops=0, name=None, space=pltpu.VMEM):
    if space == pltpu.HBM:
        args = [pltpu.with_memory_space_constraint(arg, space) for arg in args]
    return pl.pallas_call(
        kernel,
        out_shape=out_shape,
        in_specs=[pl.BlockSpec(memory_space=space)] * len(args),
        out_specs=jax.tree.map(lambda _: pl.BlockSpec(memory_space=pltpu.VMEM), out_shape),
        scratch_shapes=list(scratch),
        cost_estimate=pl.CostEstimate(flops=flops, bytes_accessed=4 * 1024 * 1024, transcendentals=0),
        compiler_params=pltpu.CompilerParams(vmem_limit_bytes=VMEM_BYTES),
        name=name,
    )(*args)


def per_device(
    right_side, face_table, send_faces, stabilize, coupling, inverse, lifting, trace_block
):
    source = right_side[0, 0]
    table = face_table[0, 0]
    send_lists = send_faces[0, 0]
    penalty = stabilize[0]
    scaling = coupling[0]
    dofs, owned = source.shape
    elements = table.shape[1]
    shared = send_lists.shape[1]
    faces = owned + 2 * shared
    shapes, trace, _ = lifting.shape
    part = shape(dofs, shared)

    pick, slab, section = call(
        first_kernel,
        (shape(owned, 2 * shared, dtype=BF16), part, part),
        source,
        send_lists,
        scratch=[
            pltpu.VMEM(source.shape, F32),
            pltpu.VMEM(send_lists.shape, jnp.int32),
            pltpu.SemaphoreType.DMA((2,)),
        ],
        name="first",
        space=pltpu.HBM,
    )
    ghosts = [passed_along(slab, "gx", 1), passed_along(section, "yz", 1)]
    turned = jnp.swapaxes(lifting, 1, 2)
    select, weights, scale = call(
        prepare_kernel,
        (
            pltpu.VMEM((faces, 4 * elements), BF16),
            shape(shapes, 2 * trace, 3 * trace, dtype=BF16),
            shape(1, 128),
        ),
        table,
        inverse,
        turned,
        trace_block,
        scratch=[
            pltpu.VMEM(table.shape, jnp.int32),
            pltpu.VMEM(inverse.shape, F32),
            pltpu.VMEM(turned.shape, F32),
            pltpu.VMEM(trace_block.shape, F32),
            pltpu.VMEM((8 * shapes, trace, 128), F32),
            pltpu.SemaphoreType.DMA((4,)),
        ],
        flops=2 * 10**9,
        name="prepare",
        space=pltpu.HBM,
    )
    odd = jnp.broadcast_to(
        jnp.stack([lax.axis_index("gx"), lax.axis_index("yz")])[:, None] % 2, (2, 128)
    ).astype(jnp.int32)
    vectors = [source]
    grams = []
    own, exchanged = source, ghosts
    for j in range(ITERS):
        final = j == ITERS - 1
        outs = [shape(8, 128), shape(dofs, owned), part, part]
        if j:
            outs = [shape(dofs, owned)] + outs
        if not final:
            outs = outs + [part] * 4
        earlier = vectors[:j] if j else []
        results = call(
            functools.partial(apply_kernel, j == 0, final, len(earlier)),
            tuple(outs),
            own,
            *exchanged,
            *earlier,
            select,
            weights,
            pick,
            penalty,
            scaling,
            scale,
            odd,
            scratch=[pltpu.VMEM((2 * dofs, faces), BF16)],
            flops=2 * 10**9,
            name=f"apply{j}",
        )
        results = list(results)
        if j:
            vectors.append(results.pop(0))
        grams.append(results.pop(0))
        own = results.pop(0)
        down = [results.pop(0) for _ in range(2)]
        if final:
            exchanged = [passed_along(down[0], "gx", -1), passed_along(down[1], "yz", -1)]
        else:
            exchanged = [exchange(results.pop(0), name) for name in STARTS] + down
    gx, yz = lax.axis_size("gx"), lax.axis_size("yz")
    rows = call(
        last_kernel,
        shape(yz, 128),
        own,
        *exchanged,
        *vectors,
        *grams,
        pick,
        scratch=[pltpu.VMEM((16, 128), F32)],
        name="last",
    )
    rows = call(add_kernel, shape(gx, 128), every(rows, "yz"), name="add")
    solution = call(solve_kernel, shape(dofs, owned), every(rows, "gx"), scale, *vectors, name="solve")
    return solution[None, None]


def solution(mesh):
    return jax.shard_map(
        per_device,
        mesh=mesh,
        in_specs=(
            P("gx", "yz", None, None),
            P("gx", "yz", None, None),
            P("gx", "yz", None, None),
            P("gx", "yz", None),
            P("gx", "yz", None),
            P(),
            P(),
            P(),
        ),
        out_specs=P("gx", "yz", None, None),
        check_vma=False,
    )
```

```python
import functools

import jax
import jax.numpy as jnp
from jax import lax
from jax.experimental import pallas as pl
from jax.experimental.pallas import tpu as pltpu
from jax.sharding import PartitionSpec as P

ITERS = 4
EPSILON = 1e-06
SHIFT = 12.0
NORM_ROOM = 1024.0
F32 = jnp.float32
BF16 = jnp.bfloat16
STARTS = ("gx later", "gx first", "yz up", "yz down")
PAIRS = [(i, j) for j in range(ITERS + 1) for i in range(j + 1)]
VMEM_BYTES = 20 * 1024 * 1024


def halves(value):
    high = value.astype(BF16)
    return high, (value - high.astype(F32)).astype(BF16)


def stacked(value):
    return jnp.concatenate(halves(value), axis=0)


def folded(value):
    half = value.shape[0] // 2
    return value[:half] + value[half:]


def dot(first, second):
    return jnp.dot(first, second, preferred_element_type=F32)


def dot_last(first, second, precision=None):
    return lax.dot_general(
        first, second, (((1,), (1,)), ((), ())), preferred_element_type=F32, precision=precision
    )


def fetched(sources, targets, semaphores):
    copies = [
        pltpu.make_async_copy(source, target, semaphores.at[k])
        for k, (source, target) in enumerate(zip(sources, targets))
    ]
    for copy in copies:
        copy.start()
    return [copy.wait for copy in copies]


def first_kernel(source_hbm, send_hbm, pick_ref, slab_ref, section_ref, source_ref, send_ref, semaphores):
    have_source, have_send = fetched((source_hbm, send_hbm), (source_ref, send_ref), semaphores)
    owned = source_ref.shape[1]
    shared = send_ref.shape[1]
    faces = lax.broadcasted_iota(jnp.int32, (owned, shared), 0)
    have_send()
    for row in range(2):
        pick_ref[:, row * shared : (row + 1) * shared] = jnp.where(
            faces == send_ref[row : row + 1, :], 1.0, 0.0
        ).astype(BF16)
    have_source()
    sent = folded(dot(stacked(source_ref[...]), pick_ref[...]))
    slab_ref[...] = sent[:, :shared]
    section_ref[...] = sent[:, shared:]


def three_pass(first, second):
    return dot_last(first[0], second[0]) + (dot_last(first[0], second[1]) + dot_last(first[1], second[0]))


def by_face(value, rows_ref, slot):
    rows, columns = value.shape
    parts = []
    for start in range(0, columns, 128):
        width = min(128, columns - start)
        rows_ref[slot, :, :width] = value[:, start : start + width]
        part = jnp.concatenate([rows_ref[slot, pl.ds(k, rows // 4, stride=4), :] for k in range(4)], axis=0)
        parts.append(part[:, :width])
        slot += 1
    return jnp.concatenate(parts, axis=1)


def columns(table_ref):
    table = table_ref[...].astype(F32)
    return jnp.concatenate([table, jnp.zeros((8 - table.shape[0], table.shape[1]), F32)], axis=0).T


def split_index(index):
    block = index // 128
    return block.astype(F32).astype(BF16), (index - block * 128).astype(F32).astype(BF16)


def prepare_kernel(
    table_hbm, send_hbm, inverse_hbm, lifting_hbm, block_hbm,
    select_ref, spread_ref, place_ref, weight_ref, scale_ref,
    table_ref, send_ref, inverse_ref, lifting_ref, block_ref, rows_ref, semaphores,
):
    have_table, have_send, have_inverse, have_lifting, have_block = fetched(
        (table_hbm, send_hbm, inverse_hbm, lifting_hbm, block_hbm),
        (table_ref, send_ref, inverse_ref, lifting_ref, block_ref),
        semaphores,
    )
    faces = select_ref.shape[0]
    elements = table_ref.shape[1]
    shapes = block_ref.shape[0]
    have_table()
    group = elements // shapes
    block, place_in = split_index(table_ref[...])
    down = lax.broadcasted_iota(jnp.int32, (128, group), 0).astype(F32).astype(BF16)
    one, zero = jnp.ones((), BF16), jnp.zeros((), BF16)
    for t in range(shapes):
        part = slice(t * group, (t + 1) * group)
        for k in range(4):
            start = (t * 4 + k) * group
            in_block = jnp.broadcast_to(block[k : k + 1, part], (128, group))
            hit = jnp.where(jnp.broadcast_to(place_in[k : k + 1, part], (128, group)) == down, one, zero)
            for b in range(faces // 128):
                select_ref[b * 128 : (b + 1) * 128, start : start + group] = jnp.where(
                    in_block == jnp.full((), b, BF16), hit, zero
                )
            spread_ref[start : start + group, :] = select_ref[:, start : start + group].T
    have_send()
    turned = columns(send_ref)
    shared, owned = turned.shape[0], place_ref.shape[1]
    lanes = lax.broadcasted_iota(jnp.int32, (shared, owned), 1).astype(F32)
    for row in range(2):
        place_ref[row * shared : (row + 1) * shared, :] = jnp.where(
            turned[:, row : row + 1] == lanes, 1.0, 0.0
        ).astype(BF16)
    block_bound = jnp.zeros((1, 1), F32)
    inner_bound = jnp.zeros((1, 1), F32)
    have_inverse()
    have_lifting()
    have_block()
    for t in range(shapes):
        lifted = halves(by_face(lifting_ref[t].T, rows_ref, 8 * t))
        inner = three_pass(halves(three_pass(lifted, halves(inverse_ref[t]))), lifted)
        block = by_face(by_face(block_ref[t], rows_ref, 8 * t + 2).T, rows_ref, 8 * t + 5)
        block_bound = jnp.maximum(block_bound, jnp.sum(block * block, keepdims=True))
        inner_bound = jnp.maximum(inner_bound, jnp.sum(inner * inner, keepdims=True))
        high, low = halves(jnp.concatenate([block, inner], axis=0))
        weight_ref[t] = jnp.concatenate([high, high, low], axis=1)
    bound = 4.0 * (6.0 + jnp.sqrt(block_bound) + 2.0 * jnp.sqrt(inner_bound)) + SHIFT
    scale_ref[...] = jnp.broadcast_to(
        jnp.maximum(1.0, bound * (1.0 / NORM_ROOM)), scale_ref.shape
    )


def inner_products(vectors, last, gram_ref, first_row):
    for i, vector in enumerate(vectors):
        gram_ref[first_row + i : first_row + i + 1, :] = lane_sums(vector * last)


def lane_sums(product):
    total = product[:, :128]
    for start in range(128, product.shape[1], 128):
        total = total + product[:, start : start + 128]
    return jnp.sum(total, axis=0, keepdims=True)


def apply_kernel(first, final, earlier, *refs):
    refs = list(refs)
    own_ref = refs.pop(0)
    if first:
        ghosts = [refs.pop(0) for _ in range(2)]
    else:
        got = [refs.pop(0) for _ in range(4)]
        down = [refs.pop(0) for _ in range(2)]
    vectors = [refs.pop(0) for _ in range(earlier)]
    select_ref, spread_ref, weight_ref, pick_ref, place_ref = refs[:5]
    stabilize_ref, coupling_ref, scale_ref, odd_ref = refs[5:9]
    refs = refs[9:]
    if not first:
        vector_ref = refs.pop(0)
    gram_ref = refs.pop(0)
    part_ref = refs.pop(0)
    down_out = [refs.pop(0) for _ in range(2)]
    if not final:
        message = [refs.pop(0) for _ in range(4)]
    (wide_ref,) = refs
    odd = odd_ref[:1, :] != 0

    dofs, owned = own_ref.shape
    shared = pick_ref.shape[1] // 2
    shapes = weight_ref.shape[0]
    elements = stabilize_ref.shape[1]
    group = elements // shapes
    trace = 4 * dofs

    if first:
        vector = own_ref[...]
        ghost = jnp.concatenate([ref[...] for ref in reversed(ghosts)], axis=1)
    else:
        parts = dict(zip(STARTS, [ref[...] for ref in got]))
        back = [jnp.where(odd, parts["gx later"], parts["gx first"]), parts["yz down"]]
        up = [jnp.where(odd, parts["gx first"], parts["gx later"]), parts["yz up"]]
        received = jnp.concatenate(back, axis=1)
        vector = own_ref[...] + folded(dot(stacked(received), place_ref[...]))
        vector_ref[...] = vector
        ghost = jnp.concatenate([a + b[...] for a, b in zip(up, down)], axis=1)
    extended = jnp.concatenate([vector, ghost], axis=1)
    wide_ref[...] = stacked(extended)

    everything = dot(wide_ref[...], select_ref[...])
    results = []
    for t in range(shapes):
        columns = slice(t * group, (t + 1) * group)
        picked = [everything[:, (t * 4 + k) * group : (t * 4 + k + 1) * group] for k in range(4)]
        high = jnp.concatenate([p[:dofs] for p in picked], axis=0)
        low = jnp.concatenate([p[dofs:] for p in picked], axis=0)
        high16, low16 = high.astype(BF16), low.astype(BF16)
        product = dot(weight_ref[t], jnp.concatenate([high16, low16, high16], axis=0))
        result = (
            stabilize_ref[:, columns] * (high + low)
            + product[:trace]
            - product[trace:] / coupling_ref[:, columns]
        )
        results += [stacked(result[k * dofs : (k + 1) * dofs]) for k in range(4)]
    inner_products([ref[...] for ref in vectors] + [vector], vector, gram_ref, 0)
    gram_ref[earlier + 1 :, :] = jnp.zeros((8 - earlier - 1, 128), F32)
    shrink = 1.0 / scale_ref[:, :1]
    summed = folded(dot(jnp.concatenate(results, axis=1), spread_ref[...])) * shrink
    part = summed[:, :owned] - (SHIFT * shrink) * vector
    part_ref[...] = part
    for i in range(2):
        down_out[i][...] = summed[:, owned + i * shared : owned + (i + 1) * shared]
    if not final:
        sent = folded(dot(stacked(part), pick_ref[...]))
        up, up_section = sent[:, :shared], sent[:, shared:]
        down, down_section = summed[:, owned : owned + shared], summed[:, owned + shared :]
        parts = {
            "gx later": jnp.where(odd, up, down),
            "gx first": jnp.where(odd, down, up),
            "yz up": up_section,
            "yz down": down_section,
        }
        for name, ref in zip(STARTS, message):
            ref[...] = parts[name]


def last_kernel(*refs):
    own_ref, slab_ref, section_ref = refs[:3]
    vectors = refs[3 : 3 + ITERS]
    grams = refs[3 + ITERS : 3 + 2 * ITERS]
    place_ref, row_ref, sums_ref = refs[3 + 2 * ITERS :]
    received = jnp.concatenate([slab_ref[...], section_ref[...]], axis=1)
    vector = own_ref[...] + folded(dot(stacked(received), place_ref[...]))
    sums_ref[...] = jnp.zeros(sums_ref.shape, F32)
    for j in range(ITERS):
        start = j * (j + 1) // 2
        sums_ref[start : start + j + 1, :] = grams[j][: j + 1, :]
    inner_products([ref[...] for ref in vectors] + [vector], vector, sums_ref, ITERS * (ITERS + 1) // 2)
    totals = jnp.sum(sums_ref[...], axis=1, keepdims=True)
    count = sums_ref.shape[0]
    diagonal = lax.broadcasted_iota(jnp.int32, (count, 128), 0) == lax.broadcasted_iota(
        jnp.int32, (count, 128), 1
    )
    row = jnp.sum(jnp.where(diagonal, totals, 0.0), axis=0, keepdims=True)
    row_ref[...] = jnp.broadcast_to(row, row_ref.shape)


def least_squares(hessenberg, target):
    breadth = len(hessenberg)
    height = len(target)
    unit_columns = []
    triangle = {}
    for k in range(breadth):
        column = list(hessenberg[k])
        for i in range(k):
            triangle[i, k] = sum(unit_columns[i][r] * column[r] for r in range(height))
            column = [column[r] - triangle[i, k] * unit_columns[i][r] for r in range(height)]
        triangle[k, k] = jnp.sqrt(sum(c * c for c in column))
        unit_columns.append([c / triangle[k, k] for c in column])
    projected = [sum(v[r] * target[r] for r in range(height)) for v in unit_columns]
    outcome = [None] * breadth
    for k in reversed(range(breadth)):
        running = projected[k]
        for i in range(k + 1, breadth):
            running = running - triangle[k, i] * outcome[i]
        outcome[k] = running / triangle[k, k]
    return outcome


def coefficients(gram, scale):
    size = ITERS + 1
    zero = jnp.zeros_like(scale)

    def inner(a, b):
        total = zero
        for i in range(size):
            for j in range(size):
                if a[i] is not None and b[j] is not None:
                    total = total + a[i] * b[j] * gram[i][j]
        return total

    def plus(a, factor, b):
        out = []
        for x, y in zip(a, b):
            if y is None:
                out.append(x)
            else:
                out.append(factor * y if x is None else x + factor * y)
        return out

    initial_norm = jnp.sqrt(gram[0][0] + EPSILON)
    krylov = [[1.0 / initial_norm] + [None] * ITERS]
    columns = []
    for j in range(ITERS):
        shifted = [None] + [scale * c if c is not None else None for c in krylov[j][:-1]]
        fresh = plus(shifted, SHIFT, krylov[j])
        products = [inner(vector, fresh) for vector in krylov]
        for value, vector in zip(products, krylov):
            fresh = plus(fresh, -value, vector)
        subdiag = jnp.sqrt(jnp.maximum(inner(fresh, fresh), 0.0) + EPSILON)
        columns.append(products + [subdiag] + [zero] * (ITERS - 1 - j))
        krylov.append([c / subdiag if c is not None else None for c in fresh])
    combine = least_squares(columns, [initial_norm] + [zero] * ITERS)
    total = [None] * size
    for y, vector in zip(combine, krylov):
        total = plus(total, y, vector)
    return total[:ITERS]


def add_kernel(rows_ref, out_ref):
    total = jnp.sum(rows_ref[...], axis=0, keepdims=True)
    out_ref[...] = jnp.broadcast_to(total, out_ref.shape)


def solve_kernel(rows_ref, scale_ref, *refs):
    vectors = refs[:ITERS]
    out_ref = refs[ITERS]
    sums = jnp.sum(rows_ref[...], axis=0, keepdims=True)
    gram = [[None] * (ITERS + 1) for _ in range(ITERS + 1)]
    for p, (i, j) in enumerate(PAIRS):
        gram[i][j] = gram[j][i] = sums[:, p : p + 1]
    weights = coefficients(gram, scale_ref[:, :1])
    total = weights[0] * vectors[0][...]
    for weight, ref in zip(weights[1:], vectors[1:]):
        total = total + weight * ref[...]
    out_ref[...] = total


def passed_along(value, axis, steps):
    count = lax.axis_size(axis)
    pairs = [(source, (source + steps) % count) for source in range(count)]
    return lax.ppermute(value, axis, pairs)


def exchange(value, name):
    axis, kind = name.split()
    if kind in ("up", "down"):
        return passed_along(value, axis, 1 if kind == "up" else -1)
    count = lax.axis_size(axis)
    ahead = 1 if kind == "later" else 0
    pairs = [(i, (i + (1 if i % 2 == ahead else -1)) % count) for i in range(count)]
    return lax.ppermute(value, axis, pairs)


def every(row, axis):
    count = row.shape[0]
    return lax.all_to_all(row.reshape(count, 1, 128), axis, 0, 0).reshape(count, 128)


def shape(*dims, dtype=F32):
    return jax.ShapeDtypeStruct(dims, dtype)


def call(kernel, out_shape, *args, scratch=(), flops=0, name=None, space=pltpu.VMEM):
    if space == pltpu.HBM:
        args = [pltpu.with_memory_space_constraint(arg, space) for arg in args]
    return pl.pallas_call(
        kernel,
        out_shape=out_shape,
        in_specs=[pl.BlockSpec(memory_space=space)] * len(args),
        out_specs=jax.tree.map(lambda _: pl.BlockSpec(memory_space=pltpu.VMEM), out_shape),
        scratch_shapes=list(scratch),
        cost_estimate=pl.CostEstimate(flops=flops, bytes_accessed=4 * 1024 * 1024, transcendentals=0),
        compiler_params=pltpu.CompilerParams(vmem_limit_bytes=VMEM_BYTES),
        name=name,
    )(*args)


def per_device(
    right_side, face_table, send_faces, stabilize, coupling, inverse, lifting, trace_block
):
    source = right_side[0, 0]
    table = face_table[0, 0]
    send_lists = send_faces[0, 0]
    penalty = stabilize[0]
    scaling = coupling[0]
    dofs, owned = source.shape
    elements = table.shape[1]
    shared = send_lists.shape[1]
    faces = owned + 2 * shared
    shapes, trace, _ = lifting.shape
    part = shape(dofs, shared)

    pick, slab, section = call(
        first_kernel,
        (shape(owned, 2 * shared, dtype=BF16), part, part),
        source,
        send_lists,
        scratch=[
            pltpu.VMEM(source.shape, F32),
            pltpu.VMEM(send_lists.shape, jnp.int32),
            pltpu.SemaphoreType.DMA((2,)),
        ],
        name="first",
        space=pltpu.HBM,
    )
    ghosts = [passed_along(section, "yz", 1), passed_along(slab, "gx", 1)]
    turned = jnp.swapaxes(lifting, 1, 2)
    select, spread, place, weights, scale = call(
        prepare_kernel,
        (
            pltpu.VMEM((faces, 4 * elements), BF16),
            pltpu.VMEM((4 * elements, faces), BF16),
            shape(2 * shared, owned, dtype=BF16),
            shape(shapes, 2 * trace, 3 * trace, dtype=BF16),
            shape(1, 128),
        ),
        table,
        send_lists,
        inverse,
        turned,
        trace_block,
        scratch=[
            pltpu.VMEM(table.shape, jnp.int32),
            pltpu.VMEM(send_lists.shape, jnp.int32),
            pltpu.VMEM(inverse.shape, F32),
            pltpu.VMEM(turned.shape, F32),
            pltpu.VMEM(trace_block.shape, F32),
            pltpu.VMEM((8 * shapes, trace, 128), F32),
            pltpu.SemaphoreType.DMA((5,)),
        ],
        flops=2 * 10**9,
        name="prepare",
        space=pltpu.HBM,
    )
    odd = jnp.broadcast_to(
        jnp.stack([lax.axis_index("gx"), lax.axis_index("yz")])[:, None] % 2, (2, 128)
    ).astype(jnp.int32)
    vectors = [source]
    grams = []
    own, exchanged = source, ghosts
    for j in range(ITERS):
        final = j == ITERS - 1
        outs = [shape(8, 128), shape(dofs, owned), part, part]
        if j:
            outs = [shape(dofs, owned)] + outs
        if not final:
            outs = outs + [part] * 4
        earlier = vectors[:j] if j else []
        results = call(
            functools.partial(apply_kernel, j == 0, final, len(earlier)),
            tuple(outs),
            own,
            *exchanged,
            *earlier,
            select,
            spread,
            weights,
            pick,
            place,
            penalty,
            scaling,
            scale,
            odd,
            scratch=[pltpu.VMEM((2 * dofs, faces), BF16)],
            flops=2 * 10**9,
            name=f"apply{j}",
        )
        results = list(results)
        if j:
            vectors.append(results.pop(0))
        grams.append(results.pop(0))
        own = results.pop(0)
        down = [results.pop(0) for _ in range(2)]
        if final:
            exchanged = [passed_along(down[0], "gx", -1), passed_along(down[1], "yz", -1)]
        else:
            exchanged = [exchange(results.pop(0), name) for name in STARTS] + down
    gx, yz = lax.axis_size("gx"), lax.axis_size("yz")
    rows = call(
        last_kernel,
        shape(yz, 128),
        own,
        *exchanged,
        *vectors,
        *grams,
        place,
        scratch=[pltpu.VMEM((16, 128), F32)],
        name="last",
    )
    rows = call(add_kernel, shape(gx, 128), every(rows, "yz"), name="add")
    solution = call(solve_kernel, shape(dofs, owned), every(rows, "gx"), scale, *vectors, name="solve")
    return solution[None, None]


def solution(mesh):
    return jax.shard_map(
        per_device,
        mesh=mesh,
        in_specs=(
            P("gx", "yz", None, None),
            P("gx", "yz", None, None),
            P("gx", "yz", None, None),
            P("gx", "yz", None),
            P("gx", "yz", None),
            P(),
            P(),
            P(),
        ),
        out_specs=P("gx", "yz", None, None),
        check_vma=False,
    )
```

```python
import functools

import jax
import jax.numpy as jnp
from jax import lax
from jax.experimental import pallas as pl
from jax.experimental.pallas import tpu as pltpu
from jax.sharding import PartitionSpec as P

ITERS = 4
EPSILON = 1e-06
SHIFT = 12.0
NORM_ROOM = 1024.0
F32 = jnp.float32
BF16 = jnp.bfloat16
STARTS = ("gx later", "gx first", "yz up", "yz down")
PAIRS = [(i, j) for j in range(ITERS + 1) for i in range(j + 1)]
VMEM_BYTES = 20 * 1024 * 1024


def halves(value):
    high = value.astype(BF16)
    return high, (value - high.astype(F32)).astype(BF16)


def stacked(value):
    return jnp.concatenate(halves(value), axis=0)


def folded(value):
    half = value.shape[0] // 2
    return value[:half] + value[half:]


def dot(first, second):
    return jnp.dot(first, second, preferred_element_type=F32)


def dot_last(first, second, precision=None):
    return lax.dot_general(
        first, second, (((1,), (1,)), ((), ())), preferred_element_type=F32, precision=precision
    )


def fetched(sources, targets, semaphores):
    copies = [
        pltpu.make_async_copy(source, target, semaphores.at[k])
        for k, (source, target) in enumerate(zip(sources, targets))
    ]
    for copy in copies:
        copy.start()
    return [copy.wait for copy in copies]


def first_kernel(source_hbm, send_hbm, slab_ref, section_ref, send_ref, source_ref, semaphores):
    have_send, have_source = fetched((send_hbm, source_hbm), (send_ref, source_ref), semaphores)
    owned = source_ref.shape[1]
    shared = send_ref.shape[1]
    faces = lax.broadcasted_iota(jnp.int32, (owned, shared), 0)
    have_send()
    pick = jnp.concatenate(
        [jnp.where(faces == send_ref[row : row + 1, :], 1.0, 0.0).astype(BF16) for row in range(2)], axis=1
    )
    have_source()
    sent = folded(dot(stacked(source_ref[...]), pick))
    slab_ref[...] = sent[:, :shared]
    section_ref[...] = sent[:, shared:]


def three_pass(first, second):
    return dot_last(first[0], second[0]) + (dot_last(first[0], second[1]) + dot_last(first[1], second[0]))


def by_face(value, rows_ref, slot):
    rows, columns = value.shape
    parts = []
    for start in range(0, columns, 128):
        width = min(128, columns - start)
        rows_ref[slot, :, :width] = value[:, start : start + width]
        part = jnp.concatenate([rows_ref[slot, pl.ds(k, rows // 4, stride=4), :] for k in range(4)], axis=0)
        parts.append(part[:, :width])
        slot += 1
    return jnp.concatenate(parts, axis=1)


def columns(table_ref):
    table = table_ref[...].astype(F32)
    return jnp.concatenate([table, jnp.zeros((8 - table.shape[0], table.shape[1]), F32)], axis=0).T


def split_index(index):
    block = index // 128
    return block.astype(F32).astype(BF16), (index - block * 128).astype(F32).astype(BF16)


def tables_kernel(
    shapes, table_hbm, send_ref, select_ref, spread_ref, meet_ref, leave_ref, place_ref, table_ref, semaphores
):
    (have_table,) = fetched((table_hbm,), (table_ref,), semaphores)
    faces = select_ref.shape[0]
    elements = table_ref.shape[1]
    sends = columns(send_ref)
    shared, owned = sends.shape[0], place_ref.shape[1]
    lanes = lax.broadcasted_iota(jnp.int32, (shared, owned), 1).astype(F32)
    for row in range(2):
        place_ref[row * shared : (row + 1) * shared, :] = jnp.where(
            sends[:, row : row + 1] == lanes, 1.0, 0.0
        ).astype(BF16)
    group = elements // shapes
    have_table()
    block, place_in = split_index(table_ref[...])
    table = table_ref[...].astype(F32)
    down = lax.broadcasted_iota(jnp.int32, (128, group), 0).astype(F32).astype(BF16)
    one, zero = jnp.ones((), BF16), jnp.zeros((), BF16)
    for t in range(shapes):
        part = slice(t * group, (t + 1) * group)
        for k in range(4):
            start = (t * 4 + k) * group
            in_block = jnp.broadcast_to(block[k : k + 1, part], (128, group))
            hit = jnp.where(jnp.broadcast_to(place_in[k : k + 1, part], (128, group)) == down, one, zero)
            for b in range(faces // 128):
                select_ref[b * 128 : (b + 1) * 128, start : start + group] = jnp.where(
                    in_block == jnp.full((), b, BF16), hit, zero
                )
            spread_ref[start : start + group, :] = select_ref[:owned, start : start + group].T
            row = table[k : k + 1, part]
            for i in range(2):
                meet_ref[i * shared : (i + 1) * shared, start : start + group] = jnp.where(
                    sends[:, i : i + 1] == row, 1.0, 0.0
                ).astype(BF16)
            meet_ref[2 * shared :, start : start + group] = select_ref[owned:, start : start + group]
            leave_ref[start : start + group, :] = meet_ref[:, start : start + group].T


def weights_kernel(inverse_ref, lifting_ref, block_ref, weight_ref, scale_ref, rows_ref):
    shapes = block_ref.shape[0]
    block_bound = jnp.zeros((1, 1), F32)
    inner_bound = jnp.zeros((1, 1), F32)
    for t in range(shapes):
        lifted = halves(by_face(lifting_ref[t].T, rows_ref, 8 * t))
        inner = three_pass(halves(three_pass(lifted, halves(inverse_ref[t]))), lifted)
        block = by_face(by_face(block_ref[t], rows_ref, 8 * t + 2).T, rows_ref, 8 * t + 5)
        block_bound = jnp.maximum(block_bound, jnp.sum(block * block, keepdims=True))
        inner_bound = jnp.maximum(inner_bound, jnp.sum(inner * inner, keepdims=True))
        high, low = halves(jnp.concatenate([block, inner], axis=0))
        weight_ref[t] = jnp.concatenate([high, high, low], axis=1)
    bound = 4.0 * (6.0 + jnp.sqrt(block_bound) + 2.0 * jnp.sqrt(inner_bound)) + SHIFT
    scale_ref[...] = jnp.broadcast_to(
        jnp.maximum(1.0, bound * (1.0 / NORM_ROOM)), scale_ref.shape
    )


def inner_products(vectors, last, gram_ref, first_row):
    for i, vector in enumerate(vectors):
        gram_ref[first_row + i : first_row + i + 1, :] = lane_sums(vector * last)


def lane_sums(product):
    total = product[:, :128]
    for start in range(128, product.shape[1], 128):
        total = total + product[:, start : start + 128]
    return jnp.sum(total, axis=0, keepdims=True)


def arrived(got, odd):
    parts = dict(zip(STARTS, [ref[...] for ref in got]))
    back = [jnp.where(odd, parts["gx later"], parts["gx first"]), parts["yz down"]]
    up = [jnp.where(odd, parts["gx first"], parts["gx later"]), parts["yz up"]]
    return back, up


def gather_kernel(source_ref, select_ref, known_ref):
    known_ref[...] = folded(dot(stacked(source_ref[...]), select_ref[: source_ref.shape[1], :]))


def step_kernel(first, final, *refs):
    refs = list(refs)
    known_ref = refs.pop(0)
    got = [refs.pop(0) for _ in range(2 if first else 4)]
    sent_before = [refs.pop(0) for _ in range(2 if first else 1)]
    meet_ref, leave_ref, weight_ref, stabilize_ref, coupling_ref, scale_ref, odd_ref = refs[:7]
    result_ref, down_ref = refs[7:9]
    odd = odd_ref[:1, :] != 0
    dofs = known_ref.shape[0]
    shared = down_ref.shape[1] // 2
    shapes = weight_ref.shape[0]
    group = stabilize_ref.shape[1] // shapes
    trace = 4 * dofs

    own = jnp.concatenate([ref[...] for ref in sent_before], axis=1)
    if first:
        section, slab = [ref[...] for ref in got]
        arrivals = jnp.concatenate([slab, section], axis=1)
        read = folded(dot(stacked(arrivals), meet_ref[2 * shared :, :]))
    else:
        back, up = arrived(got, odd)
        own = own + jnp.concatenate(back, axis=1)
        read = folded(dot(stacked(jnp.concatenate(back + up, axis=1)), meet_ref[...]))
    read = known_ref[...] + read
    for t in range(shapes):
        columns = slice(t * group, (t + 1) * group)
        values = jnp.concatenate(
            [read[:, (t * 4 + k) * group : (t * 4 + k + 1) * group] for k in range(4)], axis=0
        )
        high, low = halves(values)
        product = dot(weight_ref[t], jnp.concatenate([high, low, high], axis=0))
        result = (
            stabilize_ref[:, columns] * values + product[:trace] - product[trace:] / coupling_ref[:, columns]
        )
        for k in range(4):
            start = (t * 4 + k) * group
            result_ref[:, start : start + group] = stacked(result[k * dofs : (k + 1) * dofs])
    shrink = 1.0 / scale_ref[:, :1]
    leaving = folded(dot(result_ref[...], leave_ref[...])) * shrink
    down = [leaving[:, (2 + i) * shared : (3 + i) * shared] for i in range(2)]
    down_ref[...] = leaving[:, 2 * shared :]
    if final:
        message = dict(zip(("slab", "section"), refs[9:11]))
        message["slab"][...] = down[0]
        message["section"][...] = down[1]
        return
    sent_ref = refs[9]
    sent = leaving[:, : 2 * shared] - (SHIFT * shrink) * own
    sent_ref[...] = sent
    up = [sent[:, i * shared : (i + 1) * shared] for i in range(2)]
    parts = {
        "gx later": jnp.where(odd, up[0], down[0]),
        "gx first": jnp.where(odd, down[0], up[0]),
        "yz up": up[1],
        "yz down": down[1],
    }
    for name, ref in zip(STARTS, refs[10:]):
        ref[...] = parts[name]


def between_kernel(first, final, earlier, *refs):
    refs = list(refs)
    result_ref, own_ref = refs[:2]
    refs = refs[2:]
    if not first:
        got, refs = refs[:4], refs[4:]
    if not final:
        down_ref = refs.pop(0)
    vectors, refs = refs[:earlier], refs[earlier:]
    select_ref, spread_ref, place_ref, scale_ref, odd_ref = refs[:5]
    refs = refs[5:]
    if first:
        vector = own_ref[...]
    else:
        back, _ = arrived(got, odd_ref[:1, :] != 0)
        vector = own_ref[...] + folded(dot(stacked(jnp.concatenate(back, axis=1)), place_ref[...]))
        refs.pop(0)[...] = vector
    gram_ref, part_ref = refs[:2]
    shrink = 1.0 / scale_ref[:, :1]
    part = folded(dot(result_ref[...], spread_ref[...])) * shrink - (SHIFT * shrink) * vector
    part_ref[...] = part
    if not final:
        refs[2][...] = folded(dot(stacked(jnp.concatenate([part, down_ref[...]], axis=1)), select_ref[...]))
    inner_products([ref[...] for ref in vectors] + [vector], vector, gram_ref, 0)
    gram_ref[earlier + 1 :, :] = jnp.zeros((8 - earlier - 1, 128), F32)


def last_kernel(*refs):
    own_ref, slab_ref, section_ref = refs[:3]
    vectors = refs[3 : 3 + ITERS]
    grams = refs[3 + ITERS : 3 + 2 * ITERS]
    place_ref, row_ref, sums_ref = refs[3 + 2 * ITERS :]
    received = jnp.concatenate([slab_ref[...], section_ref[...]], axis=1)
    vector = own_ref[...] + folded(dot(stacked(received), place_ref[...]))
    sums_ref[...] = jnp.zeros(sums_ref.shape, F32)
    for j in range(ITERS):
        start = j * (j + 1) // 2
        sums_ref[start : start + j + 1, :] = grams[j][: j + 1, :]
    inner_products([ref[...] for ref in vectors] + [vector], vector, sums_ref, ITERS * (ITERS + 1) // 2)
    totals = jnp.sum(sums_ref[...], axis=1, keepdims=True)
    count = sums_ref.shape[0]
    diagonal = lax.broadcasted_iota(jnp.int32, (count, 128), 0) == lax.broadcasted_iota(
        jnp.int32, (count, 128), 1
    )
    row = jnp.sum(jnp.where(diagonal, totals, 0.0), axis=0, keepdims=True)
    row_ref[...] = jnp.broadcast_to(row, row_ref.shape)


def least_squares(hessenberg, target):
    breadth = len(hessenberg)
    height = len(target)
    unit_columns = []
    triangle = {}
    shrink = {}
    for k in range(breadth):
        column = list(hessenberg[k])
        for i in range(k):
            triangle[i, k] = sum(unit_columns[i][r] * column[r] for r in range(height))
            column = [column[r] - triangle[i, k] * unit_columns[i][r] for r in range(height)]
        square = sum(c * c for c in column)
        shrink[k] = lax.rsqrt(square)
        unit_columns.append([c * shrink[k] for c in column])
    projected = [sum(v[r] * target[r] for r in range(height)) for v in unit_columns]
    outcome = [None] * breadth
    for k in reversed(range(breadth)):
        running = projected[k]
        for i in range(k + 1, breadth):
            running = running - triangle[k, i] * outcome[i]
        outcome[k] = running * shrink[k]
    return outcome


def coefficients(gram, scale):
    size = ITERS + 1
    zero = jnp.zeros_like(scale)

    def inner(a, b):
        total = zero
        for i in range(size):
            for j in range(size):
                if a[i] is not None and b[j] is not None:
                    total = total + a[i] * b[j] * gram[i][j]
        return total

    def plus(a, factor, b):
        out = []
        for x, y in zip(a, b):
            if y is None:
                out.append(x)
            else:
                out.append(factor * y if x is None else x + factor * y)
        return out

    square = gram[0][0] + EPSILON
    initial_norm = jnp.sqrt(square)
    krylov = [[lax.rsqrt(square)] + [None] * ITERS]
    columns = []
    for j in range(ITERS):
        shifted = [None] + [scale * c if c is not None else None for c in krylov[j][:-1]]
        fresh = plus(shifted, SHIFT, krylov[j])
        products = [inner(vector, fresh) for vector in krylov]
        for value, vector in zip(products, krylov):
            fresh = plus(fresh, -value, vector)
        square = jnp.maximum(inner(fresh, fresh), 0.0) + EPSILON
        columns.append(products + [jnp.sqrt(square)] + [zero] * (ITERS - 1 - j))
        shrink = lax.rsqrt(square)
        krylov.append([c * shrink if c is not None else None for c in fresh])
    combine = least_squares(columns, [initial_norm] + [zero] * ITERS)
    total = [None] * size
    for y, vector in zip(combine, krylov):
        total = plus(total, y, vector)
    return total[:ITERS]


def add_kernel(rows_ref, out_ref):
    total = jnp.sum(rows_ref[...], axis=0, keepdims=True)
    out_ref[...] = jnp.broadcast_to(total, out_ref.shape)


def solve_kernel(rows_ref, scale_ref, *refs):
    vectors = refs[:ITERS]
    out_ref = refs[ITERS]
    sums = jnp.sum(rows_ref[...], axis=0, keepdims=True)
    gram = [[None] * (ITERS + 1) for _ in range(ITERS + 1)]
    for p, (i, j) in enumerate(PAIRS):
        gram[i][j] = gram[j][i] = sums[:, p : p + 1]
    weights = coefficients(gram, scale_ref[:, :1])
    total = weights[0] * vectors[0][...]
    for weight, ref in zip(weights[1:], vectors[1:]):
        total = total + weight * ref[...]
    out_ref[...] = total


def passed_along(value, axis, steps):
    count = lax.axis_size(axis)
    pairs = [(source, (source + steps) % count) for source in range(count)]
    return lax.ppermute(value, axis, pairs)


def exchange(value, name):
    axis, kind = name.split()
    if kind in ("up", "down"):
        return passed_along(value, axis, 1 if kind == "up" else -1)
    count = lax.axis_size(axis)
    ahead = 1 if kind == "later" else 0
    pairs = [(i, (i + (1 if i % 2 == ahead else -1)) % count) for i in range(count)]
    return lax.ppermute(value, axis, pairs)


def every(row, axis):
    count = row.shape[0]
    return lax.all_to_all(row.reshape(count, 1, 128), axis, 0, 0).reshape(count, 128)


def shape(*dims, dtype=F32):
    return jax.ShapeDtypeStruct(dims, dtype)


def call(kernel, out_shape, *args, scratch=(), flops=0, name=None, in_hbm=()):
    spaces = [pltpu.HBM if i in in_hbm else pltpu.VMEM for i in range(len(args))]
    args = [
        pltpu.with_memory_space_constraint(arg, space) if space == pltpu.HBM else arg
        for arg, space in zip(args, spaces)
    ]
    return pl.pallas_call(
        kernel,
        out_shape=out_shape,
        in_specs=[pl.BlockSpec(memory_space=space) for space in spaces],
        out_specs=jax.tree.map(lambda _: pl.BlockSpec(memory_space=pltpu.VMEM), out_shape),
        scratch_shapes=list(scratch),
        cost_estimate=pl.CostEstimate(flops=flops, bytes_accessed=4 * 1024 * 1024, transcendentals=0),
        compiler_params=pltpu.CompilerParams(vmem_limit_bytes=VMEM_BYTES),
        name=name,
    )(*args)


def per_device(
    right_side, face_table, send_faces, stabilize, coupling, inverse, lifting, trace_block
):
    source = right_side[0, 0]
    table = face_table[0, 0]
    send_lists = send_faces[0, 0]
    penalty = stabilize[0]
    scaling = coupling[0]
    dofs, owned = source.shape
    elements = table.shape[1]
    shared = send_lists.shape[1]
    faces = owned + 2 * shared
    shapes, trace, _ = lifting.shape
    part = shape(dofs, shared)

    slab, section, send_lists = call(
        first_kernel,
        (part, part, shape(*send_lists.shape, dtype=jnp.int32)),
        source,
        send_lists,
        scratch=[pltpu.VMEM(source.shape, F32), pltpu.SemaphoreType.DMA((2,))],
        name="first",
        in_hbm=(0, 1),
    )
    ghosts = [passed_along(section, "yz", 1), passed_along(slab, "gx", 1)]
    select, spread, meet, leave, place = call(
        functools.partial(tables_kernel, shapes),
        (
            pltpu.VMEM((faces, 4 * elements), BF16),
            pltpu.VMEM((4 * elements, owned), BF16),
            pltpu.VMEM((4 * shared, 4 * elements), BF16),
            pltpu.VMEM((4 * elements, 4 * shared), BF16),
            shape(2 * shared, owned, dtype=BF16),
        ),
        table,
        send_lists,
        scratch=[pltpu.VMEM(table.shape, jnp.int32), pltpu.SemaphoreType.DMA((1,))],
        flops=10**9,
        name="tables",
        in_hbm=(0,),
    )
    weights, scale = call(
        weights_kernel,
        (shape(shapes, 2 * trace, 3 * trace, dtype=BF16), shape(1, 128)),
        inverse,
        jnp.swapaxes(lifting, 1, 2),
        trace_block,
        scratch=[pltpu.VMEM((8 * shapes, trace, 128), F32)],
        flops=10**9,
        name="weights",
    )
    odd = jnp.broadcast_to(
        jnp.stack([lax.axis_index("gx"), lax.axis_index("yz")])[:, None] % 2, (2, 128)
    ).astype(jnp.int32)
    known = call(gather_kernel, shape(dofs, 4 * elements), source, select, flops=10**9, name="gather")
    vectors = [source]
    grams = []
    own, got, sent = source, ghosts, [slab, section]
    both = shape(dofs, 2 * shared)
    for j in range(ITERS):
        first, final = j == 0, j == ITERS - 1
        outs = [shape(2 * dofs, 4 * elements, dtype=BF16), both]
        results = call(
            functools.partial(step_kernel, first, final),
            tuple(outs + ([part] * 2 if final else [both] + [part] * 4)),
            known,
            *got,
            *sent,
            meet,
            leave,
            weights,
            penalty,
            scaling,
            scale,
            odd,
            flops=10**9,
            name=f"step{j}",
        )
        result, down = results[:2]
        if final:
            after = [passed_along(results[2], "gx", -1), passed_along(results[3], "yz", -1)]
        else:
            sent = [results[2]]
            after = [exchange(value, name) for value, name in zip(results[3:], STARTS)]
        earlier = vectors[:j] if j else []
        outs = [shape(8, 128), shape(dofs, owned)]
        if not first:
            outs = [shape(dofs, owned)] + outs
        if not final:
            outs = outs + [shape(dofs, 4 * elements)]
        results = list(
            call(
                functools.partial(between_kernel, first, final, len(earlier)),
                tuple(outs),
                result,
                own,
                *([] if first else got),
                *([] if final else [down]),
                *earlier,
                select,
                spread,
                place,
                scale,
                odd,
                flops=10**9,
                name=f"between{j}",
            )
        )
        if not first:
            vectors.append(results.pop(0))
        grams.append(results.pop(0))
        own = results.pop(0)
        if not final:
            known = results.pop(0)
        got = after
    gx, yz = lax.axis_size("gx"), lax.axis_size("yz")
    rows = call(
        last_kernel,
        shape(yz, 128),
        own,
        *got,
        *vectors,
        *grams,
        place,
        scratch=[pltpu.VMEM((16, 128), F32)],
        name="last",
    )
    rows = call(add_kernel, shape(gx, 128), every(rows, "yz"), name="add")
    solution = call(solve_kernel, shape(dofs, owned), every(rows, "gx"), scale, *vectors, name="solve")
    return solution[None, None]


def solution(mesh):
    return jax.shard_map(
        per_device,
        mesh=mesh,
        in_specs=(
            P("gx", "yz", None, None),
            P("gx", "yz", None, None),
            P("gx", "yz", None, None),
            P("gx", "yz", None),
            P("gx", "yz", None),
            P(),
            P(),
            P(),
        ),
        out_specs=P("gx", "yz", None, None),
        check_vma=False,
    )
```

```python
import functools

import jax
import jax.numpy as jnp
from jax import lax
from jax.experimental import pallas as pl
from jax.experimental.pallas import tpu as pltpu
from jax.sharding import PartitionSpec as P

ITERS = 4
EPSILON = 1e-06
SHIFT = 12.0
NORM_ROOM = 1024.0
F32 = jnp.float32
BF16 = jnp.bfloat16
STARTS = ("gx later", "gx first", "yz up", "yz down")
PAIRS = [(i, j) for j in range(ITERS + 1) for i in range(j + 1)]
VMEM_BYTES = 20 * 1024 * 1024


def halves(value):
    high = value.astype(BF16)
    return high, (value - high.astype(F32)).astype(BF16)


def stacked(value):
    return jnp.concatenate(halves(value), axis=0)


def folded(value):
    half = value.shape[0] // 2
    return value[:half] + value[half:]


def dot(first, second):
    return jnp.dot(first, second, preferred_element_type=F32)


def dot_last(first, second, precision=None):
    return lax.dot_general(
        first, second, (((1,), (1,)), ((), ())), preferred_element_type=F32, precision=precision
    )


def fetched(sources, targets, semaphores):
    copies = [
        pltpu.make_async_copy(source, target, semaphores.at[k])
        for k, (source, target) in enumerate(zip(sources, targets))
    ]
    for copy in copies:
        copy.start()
    return [copy.wait for copy in copies]


def first_kernel(source_hbm, send_hbm, slab_ref, section_ref, send_ref, source_ref, semaphores):
    have_send, have_source = fetched((send_hbm, source_hbm), (send_ref, source_ref), semaphores)
    owned = source_ref.shape[1]
    shared = send_ref.shape[1]
    faces = lax.broadcasted_iota(jnp.int32, (owned, shared), 0)
    have_send()
    pick = jnp.concatenate(
        [jnp.where(faces == send_ref[row : row + 1, :], 1.0, 0.0).astype(BF16) for row in range(2)], axis=1
    )
    have_source()
    sent = folded(dot(stacked(source_ref[...]), pick))
    slab_ref[...] = sent[:, :shared]
    section_ref[...] = sent[:, shared:]


def three_pass(first, second):
    return dot_last(first[0], second[0]) + (dot_last(first[0], second[1]) + dot_last(first[1], second[0]))


def by_face(value, rows_ref, slot):
    rows, columns = value.shape
    parts = []
    for start in range(0, columns, 128):
        width = min(128, columns - start)
        rows_ref[slot, :, :width] = value[:, start : start + width]
        part = jnp.concatenate([rows_ref[slot, pl.ds(k, rows // 4, stride=4), :] for k in range(4)], axis=0)
        parts.append(part[:, :width])
        slot += 1
    return jnp.concatenate(parts, axis=1)


def columns(table_ref):
    table = table_ref[...].astype(F32)
    return jnp.concatenate([table, jnp.zeros((8 - table.shape[0], table.shape[1]), F32)], axis=0).T


def split_index(index):
    block = index // 128
    return block.astype(F32).astype(BF16), (index - block * 128).astype(F32).astype(BF16)


def tables_kernel(
    shapes, table_hbm, send_ref, select_ref, spread_ref, meet_ref, leave_ref, place_ref, table_ref, semaphores
):
    (have_table,) = fetched((table_hbm,), (table_ref,), semaphores)
    faces = select_ref.shape[0]
    elements = table_ref.shape[1]
    sends = columns(send_ref)
    shared, owned = sends.shape[0], place_ref.shape[1]
    lanes = lax.broadcasted_iota(jnp.int32, (shared, owned), 1).astype(F32)
    for row in range(2):
        place_ref[row * shared : (row + 1) * shared, :] = jnp.where(
            sends[:, row : row + 1] == lanes, 1.0, 0.0
        ).astype(BF16)
    group = elements // shapes
    have_table()
    block, place_in = split_index(table_ref[...])
    table = table_ref[...].astype(F32)
    down = lax.broadcasted_iota(jnp.int32, (128, group), 0).astype(F32).astype(BF16)
    one, zero = jnp.ones((), BF16), jnp.zeros((), BF16)
    for t in range(shapes):
        part = slice(t * group, (t + 1) * group)
        for k in range(4):
            start = (t * 4 + k) * group
            in_block = jnp.broadcast_to(block[k : k + 1, part], (128, group))
            hit = jnp.where(jnp.broadcast_to(place_in[k : k + 1, part], (128, group)) == down, one, zero)
            for b in range(faces // 128):
                select_ref[b * 128 : (b + 1) * 128, start : start + group] = jnp.where(
                    in_block == jnp.full((), b, BF16), hit, zero
                )
            spread_ref[start : start + group, :] = select_ref[:owned, start : start + group].T
            row = table[k : k + 1, part]
            for i in range(2):
                meet_ref[i * shared : (i + 1) * shared, start : start + group] = jnp.where(
                    sends[:, i : i + 1] == row, 1.0, 0.0
                ).astype(BF16)
            meet_ref[2 * shared :, start : start + group] = select_ref[owned:, start : start + group]
            leave_ref[start : start + group, :] = meet_ref[:, start : start + group].T


def weights_kernel(inverse_ref, lifting_ref, block_ref, weight_ref, scale_ref, rows_ref):
    shapes = block_ref.shape[0]
    block_bound = jnp.zeros((1, 1), F32)
    inner_bound = jnp.zeros((1, 1), F32)
    for t in range(shapes):
        lifted = halves(by_face(lifting_ref[t].T, rows_ref, 8 * t))
        inner = three_pass(halves(three_pass(lifted, halves(inverse_ref[t]))), lifted)
        block = by_face(by_face(block_ref[t], rows_ref, 8 * t + 2).T, rows_ref, 8 * t + 5)
        block_bound = jnp.maximum(block_bound, jnp.sum(block * block, keepdims=True))
        inner_bound = jnp.maximum(inner_bound, jnp.sum(inner * inner, keepdims=True))
        high, low = halves(jnp.concatenate([block, inner], axis=0))
        weight_ref[t] = jnp.concatenate([high, high, low], axis=1)
    bound = 4.0 * (6.0 + jnp.sqrt(block_bound) + 2.0 * jnp.sqrt(inner_bound)) + SHIFT
    scale_ref[...] = jnp.broadcast_to(
        jnp.maximum(1.0, bound * (1.0 / NORM_ROOM)), scale_ref.shape
    )


def inner_products(vectors, last, gram_ref, first_row):
    for i, vector in enumerate(vectors):
        gram_ref[first_row + i : first_row + i + 1, :] = lane_sums(vector * last)


def lane_sums(product):
    total = product[:, :128]
    for start in range(128, product.shape[1], 128):
        total = total + product[:, start : start + 128]
    return jnp.sum(total, axis=0, keepdims=True)


def arrived(got, odd):
    parts = dict(zip(STARTS, [ref[...] for ref in got]))
    back = [jnp.where(odd, parts["gx later"], parts["gx first"]), parts["yz down"]]
    up = [jnp.where(odd, parts["gx first"], parts["gx later"]), parts["yz up"]]
    return back, up


def gather_kernel(source_ref, select_ref, known_ref):
    known_ref[...] = folded(dot(stacked(source_ref[...]), select_ref[: source_ref.shape[1], :]))


def step_kernel(first, final, *refs):
    refs = list(refs)
    known_ref = refs.pop(0)
    got = [refs.pop(0) for _ in range(2 if first else 4)]
    sent_before = [refs.pop(0) for _ in range(2 if first else 1)]
    meet_ref, leave_ref, weight_ref, stabilize_ref, coupling_ref, scale_ref, odd_ref = refs[:7]
    result_ref = refs[7]
    odd = odd_ref[:1, :] != 0
    dofs = known_ref.shape[0]
    shared = leave_ref.shape[1] // 4
    shapes = weight_ref.shape[0]
    group = stabilize_ref.shape[1] // shapes
    trace = 4 * dofs

    own = jnp.concatenate([ref[...] for ref in sent_before], axis=1)
    if first:
        section, slab = [ref[...] for ref in got]
        arrivals = jnp.concatenate([slab, section], axis=1)
        read = folded(dot(stacked(arrivals), meet_ref[2 * shared :, :]))
    else:
        back, up = arrived(got, odd)
        own = own + jnp.concatenate(back, axis=1)
        read = folded(dot(stacked(jnp.concatenate(back + up, axis=1)), meet_ref[...]))
    read = known_ref[...] + read
    for t in range(shapes):
        columns = slice(t * group, (t + 1) * group)
        values = jnp.concatenate(
            [read[:, (t * 4 + k) * group : (t * 4 + k + 1) * group] for k in range(4)], axis=0
        )
        high, low = halves(values)
        product = dot(weight_ref[t], jnp.concatenate([high, low, high], axis=0))
        result = (
            stabilize_ref[:, columns] * values + product[:trace] - product[trace:] / coupling_ref[:, columns]
        )
        for k in range(4):
            start = (t * 4 + k) * group
            result_ref[:, start : start + group] = stacked(result[k * dofs : (k + 1) * dofs])
    shrink = 1.0 / scale_ref[:, :1]
    if final:
        leaving = folded(dot(result_ref[...], leave_ref[:, 2 * shared :])) * shrink
        for i in range(2):
            refs[8 + i][...] = leaving[:, i * shared : (i + 1) * shared]
        return
    down_ref, sent_ref = refs[8:10]
    leaving = folded(dot(result_ref[...], leave_ref[...])) * shrink
    down = [leaving[:, (2 + i) * shared : (3 + i) * shared] for i in range(2)]
    down_ref[...] = leaving[:, 2 * shared :]
    sent = leaving[:, : 2 * shared] - (SHIFT * shrink) * own
    sent_ref[...] = sent
    up = [sent[:, i * shared : (i + 1) * shared] for i in range(2)]
    parts = {
        "gx later": jnp.where(odd, up[0], down[0]),
        "gx first": jnp.where(odd, down[0], up[0]),
        "yz up": up[1],
        "yz down": down[1],
    }
    for name, ref in zip(STARTS, refs[10:]):
        ref[...] = parts[name]


def between_kernel(first, final, earlier, *refs):
    refs = list(refs)
    result_ref, own_ref = refs[:2]
    refs = refs[2:]
    if not first:
        got, refs = refs[:4], refs[4:]
    if not final:
        down_ref = refs.pop(0)
    vectors, refs = refs[:earlier], refs[earlier:]
    select_ref, spread_ref, place_ref, scale_ref, odd_ref = refs[:5]
    refs = refs[5:]
    if first:
        vector = own_ref[...]
    else:
        back, _ = arrived(got, odd_ref[:1, :] != 0)
        vector = own_ref[...] + folded(dot(stacked(jnp.concatenate(back, axis=1)), place_ref[...]))
        refs.pop(0)[...] = vector
    gram_ref, part_ref = refs[:2]
    shrink = 1.0 / scale_ref[:, :1]
    part = folded(dot(result_ref[...], spread_ref[...])) * shrink - (SHIFT * shrink) * vector
    part_ref[...] = part
    if not final:
        refs[2][...] = folded(dot(stacked(jnp.concatenate([part, down_ref[...]], axis=1)), select_ref[...]))
    inner_products([ref[...] for ref in vectors] + [vector], vector, gram_ref, 0)
    gram_ref[earlier + 1 :, :] = jnp.zeros((8 - earlier - 1, 128), F32)


def last_kernel(*refs):
    own_ref, slab_ref, section_ref = refs[:3]
    vectors = refs[3 : 3 + ITERS]
    grams = refs[3 + ITERS : 3 + 2 * ITERS]
    place_ref, row_ref, sums_ref = refs[3 + 2 * ITERS :]
    received = jnp.concatenate([slab_ref[...], section_ref[...]], axis=1)
    vector = own_ref[...] + folded(dot(stacked(received), place_ref[...]))
    sums_ref[...] = jnp.zeros(sums_ref.shape, F32)
    for j in range(ITERS):
        start = j * (j + 1) // 2
        sums_ref[start : start + j + 1, :] = grams[j][: j + 1, :]
    inner_products([ref[...] for ref in vectors] + [vector], vector, sums_ref, ITERS * (ITERS + 1) // 2)
    totals = jnp.sum(sums_ref[...], axis=1, keepdims=True)
    count = sums_ref.shape[0]
    diagonal = lax.broadcasted_iota(jnp.int32, (count, 128), 0) == lax.broadcasted_iota(
        jnp.int32, (count, 128), 1
    )
    row = jnp.sum(jnp.where(diagonal, totals, 0.0), axis=0, keepdims=True)
    row_ref[...] = jnp.broadcast_to(row, row_ref.shape)


def added(terms):
    terms = list(terms)
    while len(terms) > 1:
        terms = [a + b for a, b in zip(terms[::2], terms[1::2])] + terms[len(terms) // 2 * 2 :]
    return terms[0]


def least_squares(hessenberg, target):
    breadth = len(hessenberg)
    height = len(target)
    unit_columns = []
    triangle = {}
    shrink = {}
    for k in range(breadth):
        column = list(hessenberg[k])
        for i in range(k):
            triangle[i, k] = added(unit_columns[i][r] * column[r] for r in range(height))
            column = [column[r] - triangle[i, k] * unit_columns[i][r] for r in range(height)]
        square = added(c * c for c in column)
        shrink[k] = lax.rsqrt(square)
        unit_columns.append([c * shrink[k] for c in column])
    projected = [added(v[r] * target[r] for r in range(height)) for v in unit_columns]
    outcome = [None] * breadth
    for k in reversed(range(breadth)):
        running = projected[k]
        for i in range(k + 1, breadth):
            running = running - triangle[k, i] * outcome[i]
        outcome[k] = running * shrink[k]
    return outcome


def coefficients(gram, scale):
    size = ITERS + 1
    zero = jnp.zeros_like(scale)

    def inner(a, b):
        rows = [(x, row) for x, row in zip(a, gram) if x is not None]
        return added(x * added(y * g for y, g in zip(b, row) if y is not None) for x, row in rows)

    def plus(a, factor, b):
        out = []
        for x, y in zip(a, b):
            if y is None:
                out.append(x)
            else:
                out.append(factor * y if x is None else x + factor * y)
        return out

    square = gram[0][0] + EPSILON
    initial_norm = jnp.sqrt(square)
    krylov = [[lax.rsqrt(square)] + [None] * ITERS]
    columns = []
    for j in range(ITERS):
        shifted = [None] + [scale * c if c is not None else None for c in krylov[j][:-1]]
        fresh = plus(shifted, SHIFT, krylov[j])
        products = [inner(vector, fresh) for vector in krylov]
        for value, vector in zip(products, krylov):
            fresh = plus(fresh, -value, vector)
        square = jnp.maximum(inner(fresh, fresh), 0.0) + EPSILON
        columns.append(products + [jnp.sqrt(square)] + [zero] * (ITERS - 1 - j))
        shrink = lax.rsqrt(square)
        krylov.append([c * shrink if c is not None else None for c in fresh])
    combine = least_squares(columns, [initial_norm] + [zero] * ITERS)
    total = [None] * size
    for y, vector in zip(combine, krylov):
        total = plus(total, y, vector)
    return total[:ITERS]


def add_kernel(rows_ref, out_ref):
    total = jnp.sum(rows_ref[...], axis=0, keepdims=True)
    out_ref[...] = jnp.broadcast_to(total, out_ref.shape)


def solve_kernel(rows_ref, scale_ref, *refs):
    vectors = refs[:ITERS]
    out_ref = refs[ITERS]
    sums = jnp.sum(rows_ref[...], axis=0, keepdims=True)
    gram = [[None] * (ITERS + 1) for _ in range(ITERS + 1)]
    for p, (i, j) in enumerate(PAIRS):
        gram[i][j] = gram[j][i] = sums[:, p : p + 1]
    weights = coefficients(gram, scale_ref[:, :1])
    total = weights[0] * vectors[0][...]
    for weight, ref in zip(weights[1:], vectors[1:]):
        total = total + weight * ref[...]
    out_ref[...] = total


def passed_along(value, axis, steps):
    count = lax.axis_size(axis)
    pairs = [(source, (source + steps) % count) for source in range(count)]
    return lax.ppermute(value, axis, pairs)


def exchange(value, name):
    axis, kind = name.split()
    if kind in ("up", "down"):
        return passed_along(value, axis, 1 if kind == "up" else -1)
    count = lax.axis_size(axis)
    ahead = 1 if kind == "later" else 0
    pairs = [(i, (i + (1 if i % 2 == ahead else -1)) % count) for i in range(count)]
    return lax.ppermute(value, axis, pairs)


def every(row, axis):
    count = row.shape[0]
    return lax.all_to_all(row.reshape(count, 1, 128), axis, 0, 0).reshape(count, 128)


def shape(*dims, dtype=F32):
    return jax.ShapeDtypeStruct(dims, dtype)


def call(kernel, out_shape, *args, scratch=(), flops=0, name=None, in_hbm=()):
    spaces = [pltpu.HBM if i in in_hbm else pltpu.VMEM for i in range(len(args))]
    args = [
        pltpu.with_memory_space_constraint(arg, space) if space == pltpu.HBM else arg
        for arg, space in zip(args, spaces)
    ]
    return pl.pallas_call(
        kernel,
        out_shape=out_shape,
        in_specs=[pl.BlockSpec(memory_space=space) for space in spaces],
        out_specs=jax.tree.map(lambda _: pl.BlockSpec(memory_space=pltpu.VMEM), out_shape),
        scratch_shapes=list(scratch),
        cost_estimate=pl.CostEstimate(flops=flops, bytes_accessed=4 * 1024 * 1024, transcendentals=0),
        compiler_params=pltpu.CompilerParams(vmem_limit_bytes=VMEM_BYTES),
        name=name,
    )(*args)


def per_device(
    right_side, face_table, send_faces, stabilize, coupling, inverse, lifting, trace_block
):
    source = right_side[0, 0]
    table = face_table[0, 0]
    send_lists = send_faces[0, 0]
    penalty = stabilize[0]
    scaling = coupling[0]
    dofs, owned = source.shape
    elements = table.shape[1]
    shared = send_lists.shape[1]
    faces = owned + 2 * shared
    shapes, trace, _ = lifting.shape
    part = shape(dofs, shared)

    slab, section, send_lists = call(
        first_kernel,
        (part, part, shape(*send_lists.shape, dtype=jnp.int32)),
        source,
        send_lists,
        scratch=[pltpu.VMEM(source.shape, F32), pltpu.SemaphoreType.DMA((2,))],
        name="first",
        in_hbm=(0, 1),
    )
    ghosts = [passed_along(section, "yz", 1), passed_along(slab, "gx", 1)]
    select, spread, meet, leave, place = call(
        functools.partial(tables_kernel, shapes),
        (
            pltpu.VMEM((faces, 4 * elements), BF16),
            pltpu.VMEM((4 * elements, owned), BF16),
            pltpu.VMEM((4 * shared, 4 * elements), BF16),
            pltpu.VMEM((4 * elements, 4 * shared), BF16),
            shape(2 * shared, owned, dtype=BF16),
        ),
        table,
        send_lists,
        scratch=[pltpu.VMEM(table.shape, jnp.int32), pltpu.SemaphoreType.DMA((1,))],
        flops=10**9,
        name="tables",
        in_hbm=(0,),
    )
    weights, scale = call(
        weights_kernel,
        (shape(shapes, 2 * trace, 3 * trace, dtype=BF16), shape(1, 128)),
        inverse,
        jnp.swapaxes(lifting, 1, 2),
        trace_block,
        scratch=[pltpu.VMEM((8 * shapes, trace, 128), F32)],
        flops=10**9,
        name="weights",
    )
    odd = jnp.broadcast_to(
        jnp.stack([lax.axis_index("gx"), lax.axis_index("yz")])[:, None] % 2, (2, 128)
    ).astype(jnp.int32)
    known = call(gather_kernel, shape(dofs, 4 * elements), source, select, flops=10**9, name="gather")
    vectors = [source]
    grams = []
    own, got, sent = source, ghosts, [slab, section]
    both = shape(dofs, 2 * shared)
    for j in range(ITERS):
        first, final = j == 0, j == ITERS - 1
        outs = [shape(2 * dofs, 4 * elements, dtype=BF16)]
        results = call(
            functools.partial(step_kernel, first, final),
            tuple(outs + ([part] * 2 if final else [both] * 2 + [part] * 4)),
            known,
            *got,
            *sent,
            meet,
            leave,
            weights,
            penalty,
            scaling,
            scale,
            odd,
            flops=10**9,
            name=f"step{j}",
        )
        result = results[0]
        if final:
            after = [passed_along(results[1], "gx", -1), passed_along(results[2], "yz", -1)]
        else:
            down, sent = results[1], [results[2]]
            after = [exchange(value, name) for value, name in zip(results[3:], STARTS)]
        earlier = vectors[:j] if j else []
        outs = [shape(8, 128), shape(dofs, owned)]
        if not first:
            outs = [shape(dofs, owned)] + outs
        if not final:
            outs = outs + [shape(dofs, 4 * elements)]
        results = list(
            call(
                functools.partial(between_kernel, first, final, len(earlier)),
                tuple(outs),
                result,
                own,
                *([] if first else got),
                *([] if final else [down]),
                *earlier,
                select,
                spread,
                place,
                scale,
                odd,
                flops=10**9,
                name=f"between{j}",
            )
        )
        if not first:
            vectors.append(results.pop(0))
        grams.append(results.pop(0))
        own = results.pop(0)
        if not final:
            known = results.pop(0)
        got = after
    gx, yz = lax.axis_size("gx"), lax.axis_size("yz")
    rows = call(
        last_kernel,
        shape(yz, 128),
        own,
        *got,
        *vectors,
        *grams,
        place,
        scratch=[pltpu.VMEM((16, 128), F32)],
        name="last",
    )
    rows = call(add_kernel, shape(gx, 128), every(rows, "yz"), name="add")
    solution = call(solve_kernel, shape(dofs, owned), every(rows, "gx"), scale, *vectors, name="solve")
    return solution[None, None]


def solution(mesh):
    return jax.shard_map(
        per_device,
        mesh=mesh,
        in_specs=(
            P("gx", "yz", None, None),
            P("gx", "yz", None, None),
            P("gx", "yz", None, None),
            P("gx", "yz", None),
            P("gx", "yz", None),
            P(),
            P(),
            P(),
        ),
        out_specs=P("gx", "yz", None, None),
        check_vma=False,
    )
```

```python
import functools

import jax
import jax.numpy as jnp
from jax import lax
from jax.experimental import pallas as pl
from jax.experimental.pallas import tpu as pltpu
from jax.sharding import PartitionSpec as P

ITERS = 4
EPSILON = 1e-06
SHIFT = 12.0
NORM_ROOM = 1024.0
F32 = jnp.float32
BF16 = jnp.bfloat16
STARTS = ("gx later", "gx first", "yz up", "yz down")
PAIRS = [(i, j) for j in range(ITERS + 1) for i in range(j + 1)]
VMEM_BYTES = 20 * 1024 * 1024


def halves(value):
    high = value.astype(BF16)
    return high, (value - high.astype(F32)).astype(BF16)


def stacked(value):
    return jnp.concatenate(halves(value), axis=0)


def folded(value):
    half = value.shape[0] // 2
    return value[:half] + value[half:]


def dot(first, second):
    return jnp.dot(first, second, preferred_element_type=F32)


def dot_last(first, second, precision=None):
    return lax.dot_general(
        first, second, (((1,), (1,)), ((), ())), preferred_element_type=F32, precision=precision
    )


def fetched(sources, targets, semaphores):
    copies = [
        pltpu.make_async_copy(source, target, semaphores.at[k])
        for k, (source, target) in enumerate(zip(sources, targets))
    ]
    for copy in copies:
        copy.start()
    return [copy.wait for copy in copies]


def first_kernel(source_hbm, send_hbm, slab_ref, section_ref, send_ref, source_ref, semaphores):
    have_send, have_source = fetched((send_hbm, source_hbm), (send_ref, source_ref), semaphores)
    owned = source_ref.shape[1]
    shared = send_ref.shape[1]
    faces = lax.broadcasted_iota(jnp.int32, (owned, shared), 0)
    have_send()
    pick = jnp.concatenate(
        [jnp.where(faces == send_ref[row : row + 1, :], 1.0, 0.0).astype(BF16) for row in range(2)], axis=1
    )
    have_source()
    sent = folded(dot(stacked(source_ref[...]), pick))
    slab_ref[...] = sent[:, :shared]
    section_ref[...] = sent[:, shared:]


def three_pass(first, second):
    return dot_last(first[0], second[0]) + (dot_last(first[0], second[1]) + dot_last(first[1], second[0]))


def by_face(value, rows_ref, slot):
    rows, columns = value.shape
    parts = []
    for start in range(0, columns, 128):
        width = min(128, columns - start)
        rows_ref[slot, :, :width] = value[:, start : start + width]
        part = jnp.concatenate([rows_ref[slot, pl.ds(k, rows // 4, stride=4), :] for k in range(4)], axis=0)
        parts.append(part[:, :width])
        slot += 1
    return jnp.concatenate(parts, axis=1)


def columns(table_ref):
    table = table_ref[...].astype(F32)
    return jnp.concatenate([table, jnp.zeros((8 - table.shape[0], table.shape[1]), F32)], axis=0).T


def split_index(index):
    block = index // 128
    return block.astype(F32).astype(BF16), (index - block * 128).astype(F32).astype(BF16)


def tables_kernel(
    shapes, table_hbm, inverse_hbm, lifting_hbm, block_hbm, send_ref,
    select_ref, spread_ref, meet_ref, leave_ref, place_ref, inverse_ref, lifting_ref, block_ref, table_ref, semaphores,
):
    have_table, *have_weights = fetched(
        (table_hbm, block_hbm, lifting_hbm, inverse_hbm), (table_ref, block_ref, lifting_ref, inverse_ref), semaphores
    )
    faces = select_ref.shape[0]
    elements = table_ref.shape[1]
    sends = columns(send_ref)
    shared, owned = sends.shape[0], place_ref.shape[1]
    lanes = lax.broadcasted_iota(jnp.int32, (shared, owned), 1).astype(F32)
    for row in range(2):
        place_ref[row * shared : (row + 1) * shared, :] = jnp.where(
            sends[:, row : row + 1] == lanes, 1.0, 0.0
        ).astype(BF16)
    group = elements // shapes
    have_table()
    block, place_in = split_index(table_ref[...])
    table = table_ref[...].astype(F32)
    down = lax.broadcasted_iota(jnp.int32, (128, group), 0).astype(F32).astype(BF16)
    one, zero = jnp.ones((), BF16), jnp.zeros((), BF16)
    for t in range(shapes):
        part = slice(t * group, (t + 1) * group)
        for k in range(4):
            start = (t * 4 + k) * group
            in_block = jnp.broadcast_to(block[k : k + 1, part], (128, group))
            hit = jnp.where(jnp.broadcast_to(place_in[k : k + 1, part], (128, group)) == down, one, zero)
            for b in range(faces // 128):
                select_ref[b * 128 : (b + 1) * 128, start : start + group] = jnp.where(
                    in_block == jnp.full((), b, BF16), hit, zero
                )
            spread_ref[start : start + group, :] = select_ref[:owned, start : start + group].T
            row = table[k : k + 1, part]
            for i in range(2):
                meet_ref[i * shared : (i + 1) * shared, start : start + group] = jnp.where(
                    sends[:, i : i + 1] == row, 1.0, 0.0
                ).astype(BF16)
            meet_ref[2 * shared :, start : start + group] = select_ref[owned:, start : start + group]
            leave_ref[start : start + group, :] = meet_ref[:, start : start + group].T
    for have in have_weights:
        have()


def weights_kernel(inverse_ref, lifting_ref, block_ref, weight_ref, scale_ref, rows_ref):
    shapes = block_ref.shape[0]
    block_bound = jnp.zeros((1, 1), F32)
    inner_bound = jnp.zeros((1, 1), F32)
    for t in range(shapes):
        lifted = halves(by_face(lifting_ref[t].T, rows_ref, 8 * t))
        inner = three_pass(halves(three_pass(lifted, halves(inverse_ref[t]))), lifted)
        block = by_face(by_face(block_ref[t], rows_ref, 8 * t + 2).T, rows_ref, 8 * t + 5)
        block_bound = jnp.maximum(block_bound, jnp.sum(block * block, keepdims=True))
        inner_bound = jnp.maximum(inner_bound, jnp.sum(inner * inner, keepdims=True))
        high, low = halves(jnp.concatenate([block, inner], axis=0))
        weight_ref[t] = jnp.concatenate([high, high, low], axis=1)
    bound = 4.0 * (6.0 + jnp.sqrt(block_bound) + 2.0 * jnp.sqrt(inner_bound)) + SHIFT
    scale_ref[...] = jnp.broadcast_to(
        jnp.maximum(1.0, bound * (1.0 / NORM_ROOM)), scale_ref.shape
    )


def inner_products(vectors, last, gram_ref, first_row):
    for i, vector in enumerate(vectors):
        gram_ref[first_row + i : first_row + i + 1, :] = lane_sums(vector * last)


def lane_sums(product):
    total = product[:, :128]
    for start in range(128, product.shape[1], 128):
        total = total + product[:, start : start + 128]
    return jnp.sum(total, axis=0, keepdims=True)


def arrived(got, odd):
    parts = dict(zip(STARTS, [ref[...] for ref in got]))
    back = [jnp.where(odd, parts["gx later"], parts["gx first"]), parts["yz down"]]
    up = [jnp.where(odd, parts["gx first"], parts["gx later"]), parts["yz up"]]
    return back, up


def gather_kernel(source_ref, select_ref, known_ref):
    known_ref[...] = folded(dot(stacked(source_ref[...]), select_ref[: source_ref.shape[1], :]))


def step_kernel(first, final, *refs):
    refs = list(refs)
    known_ref = refs.pop(0)
    got = [refs.pop(0) for _ in range(2 if first else 4)]
    sent_before = [refs.pop(0) for _ in range(2 if first else 1)]
    meet_ref, leave_ref, weight_ref, stabilize_ref, coupling_ref, scale_ref, odd_ref = refs[:7]
    result_ref = refs[7]
    odd = odd_ref[:1, :] != 0
    dofs = known_ref.shape[0]
    shared = leave_ref.shape[1] // 4
    shapes = weight_ref.shape[0]
    group = stabilize_ref.shape[1] // shapes
    trace = 4 * dofs

    own = jnp.concatenate([ref[...] for ref in sent_before], axis=1)
    if first:
        section, slab = [ref[...] for ref in got]
        arrivals = jnp.concatenate([slab, section], axis=1)
        read = folded(dot(stacked(arrivals), meet_ref[2 * shared :, :]))
    else:
        back, up = arrived(got, odd)
        own = own + jnp.concatenate(back, axis=1)
        read = folded(dot(stacked(jnp.concatenate(back + up, axis=1)), meet_ref[...]))
    read = known_ref[...] + read
    for t in range(shapes):
        columns = slice(t * group, (t + 1) * group)
        values = jnp.concatenate(
            [read[:, (t * 4 + k) * group : (t * 4 + k + 1) * group] for k in range(4)], axis=0
        )
        high, low = halves(values)
        product = dot(weight_ref[t], jnp.concatenate([high, low, high], axis=0))
        result = (
            stabilize_ref[:, columns] * values + product[:trace] - product[trace:] / coupling_ref[:, columns]
        )
        for k in range(4):
            start = (t * 4 + k) * group
            result_ref[:, start : start + group] = stacked(result[k * dofs : (k + 1) * dofs])
    shrink = 1.0 / scale_ref[:, :1]
    if final:
        leaving = folded(dot(result_ref[...], leave_ref[:, shared : 3 * shared])) * shrink
        refs[8][...] = leaving[:, shared:]
        refs[9][...] = leaving[:, :shared] - (SHIFT * shrink) * own[:, shared:]
        return
    down_ref, sent_ref = refs[8:10]
    leaving = folded(dot(result_ref[...], leave_ref[...])) * shrink
    down = [leaving[:, (2 + i) * shared : (3 + i) * shared] for i in range(2)]
    down_ref[...] = leaving[:, 2 * shared :]
    sent = leaving[:, : 2 * shared] - (SHIFT * shrink) * own
    sent_ref[...] = sent
    up = [sent[:, i * shared : (i + 1) * shared] for i in range(2)]
    parts = {
        "gx later": jnp.where(odd, up[0], down[0]),
        "gx first": jnp.where(odd, down[0], up[0]),
        "yz up": up[1],
        "yz down": down[1],
    }
    for name, ref in zip(STARTS, refs[10:]):
        ref[...] = parts[name]


def between_kernel(first, final, earlier, *refs):
    refs = list(refs)
    result_ref, own_ref = refs[:2]
    refs = refs[2:]
    if not first:
        got, refs = refs[:4], refs[4:]
    if not final:
        down_ref = refs.pop(0)
    vectors, refs = refs[:earlier], refs[earlier:]
    select_ref, spread_ref, place_ref, scale_ref, odd_ref = refs[:5]
    refs = refs[5:]
    if final:
        leave_ref = refs.pop(0)
    if first:
        vector = own_ref[...]
    else:
        back, _ = arrived(got, odd_ref[:1, :] != 0)
        vector = own_ref[...] + folded(dot(stacked(jnp.concatenate(back, axis=1)), place_ref[...]))
        refs.pop(0)[...] = vector
    gram_ref, part_ref = refs[:2]
    shrink = 1.0 / scale_ref[:, :1]
    part = folded(dot(result_ref[...], spread_ref[...])) * shrink - (SHIFT * shrink) * vector
    part_ref[...] = part
    if final:
        ghost = leave_ref[:, 3 * leave_ref.shape[1] // 4 :]
        refs[2][...] = folded(dot(result_ref[...], ghost)) * shrink
    else:
        refs[2][...] = folded(dot(stacked(jnp.concatenate([part, down_ref[...]], axis=1)), select_ref[...]))
    inner_products([ref[...] for ref in vectors] + [vector], vector, gram_ref, 0)
    gram_ref[earlier + 1 :, :] = jnp.zeros((8 - earlier - 1, 128), F32)


def last_kernel(*refs):
    refs = list(refs)
    own_ref, slab_ref, section_ref, ghost_ref = [refs.pop(0) for _ in range(4)]
    vectors = [refs.pop(0) for _ in range(ITERS)]
    grams = [refs.pop(0) for _ in range(ITERS)]
    ghosts = [refs.pop(0)[...]]
    for _ in range(1, ITERS):
        arrived_ref, sums_ref = refs.pop(0), refs.pop(0)
        shared = arrived_ref.shape[1]
        ghosts.append(arrived_ref[...] + sums_ref[:, shared:])
    place_ref, row_ref, sums_ref = refs
    vector = own_ref[...] + folded(dot(stacked(slab_ref[...]), place_ref[:shared, :]))
    sent_along_yz = jnp.sum(place_ref[shared:, :].astype(F32), axis=0, keepdims=True)
    vector = jnp.where(sent_along_yz > 0.5, 0.0, vector)
    ghost = ghost_ref[...] + section_ref[...]
    sums_ref[...] = jnp.zeros(sums_ref.shape, F32)
    for j in range(ITERS):
        start = j * (j + 1) // 2
        sums_ref[start : start + j + 1, :] = grams[j][: j + 1, :]
    start = ITERS * (ITERS + 1) // 2
    for i, (whole, part) in enumerate(zip([ref[...] for ref in vectors] + [vector], ghosts + [ghost])):
        sums_ref[start + i : start + i + 1, :] = lane_sums(whole * vector) + lane_sums(part * ghost)
    totals = jnp.sum(sums_ref[...], axis=1, keepdims=True)
    count = sums_ref.shape[0]
    diagonal = lax.broadcasted_iota(jnp.int32, (count, 128), 0) == lax.broadcasted_iota(
        jnp.int32, (count, 128), 1
    )
    row = jnp.sum(jnp.where(diagonal, totals, 0.0), axis=0, keepdims=True)
    row_ref[...] = jnp.broadcast_to(row, row_ref.shape)


def added(terms):
    terms = list(terms)
    while len(terms) > 1:
        terms = [a + b for a, b in zip(terms[::2], terms[1::2])] + terms[len(terms) // 2 * 2 :]
    return terms[0]


def least_squares(hessenberg, target):
    breadth = len(hessenberg)
    height = len(target)
    unit_columns = []
    triangle = {}
    shrink = {}
    for k in range(breadth):
        column = list(hessenberg[k])
        for i in range(k):
            triangle[i, k] = added(unit_columns[i][r] * column[r] for r in range(height))
            column = [column[r] - triangle[i, k] * unit_columns[i][r] for r in range(height)]
        square = added(c * c for c in column)
        shrink[k] = lax.rsqrt(square)
        unit_columns.append([c * shrink[k] for c in column])
    projected = [added(v[r] * target[r] for r in range(height)) for v in unit_columns]
    outcome = [None] * breadth
    for k in reversed(range(breadth)):
        running = projected[k]
        for i in range(k + 1, breadth):
            running = running - triangle[k, i] * outcome[i]
        outcome[k] = running * shrink[k]
    return outcome


def coefficients(gram, scale):
    size = ITERS + 1
    zero = jnp.zeros_like(scale)

    def inner(a, b):
        rows = [(x, row) for x, row in zip(a, gram) if x is not None]
        return added(x * added(y * g for y, g in zip(b, row) if y is not None) for x, row in rows)

    def plus(a, factor, b):
        out = []
        for x, y in zip(a, b):
            if y is None:
                out.append(x)
            else:
                out.append(factor * y if x is None else x + factor * y)
        return out

    square = gram[0][0] + EPSILON
    initial_norm = jnp.sqrt(square)
    krylov = [[lax.rsqrt(square)] + [None] * ITERS]
    columns = []
    for j in range(ITERS):
        shifted = [None] + [scale * c if c is not None else None for c in krylov[j][:-1]]
        fresh = plus(shifted, SHIFT, krylov[j])
        products = [inner(vector, fresh) for vector in krylov]
        for value, vector in zip(products, krylov):
            fresh = plus(fresh, -value, vector)
        square = jnp.maximum(inner(fresh, fresh), 0.0) + EPSILON
        columns.append(products + [jnp.sqrt(square)] + [zero] * (ITERS - 1 - j))
        shrink = lax.rsqrt(square)
        krylov.append([c * shrink if c is not None else None for c in fresh])
    combine = least_squares(columns, [initial_norm] + [zero] * ITERS)
    total = [None] * size
    for y, vector in zip(combine, krylov):
        total = plus(total, y, vector)
    return total[:ITERS]


def add_kernel(rows_ref, out_ref):
    total = jnp.sum(rows_ref[...], axis=0, keepdims=True)
    out_ref[...] = jnp.broadcast_to(total, out_ref.shape)


def solve_kernel(rows_ref, scale_ref, *refs):
    vectors = refs[:ITERS]
    out_ref = refs[ITERS]
    sums = jnp.sum(rows_ref[...], axis=0, keepdims=True)
    gram = [[None] * (ITERS + 1) for _ in range(ITERS + 1)]
    for p, (i, j) in enumerate(PAIRS):
        gram[i][j] = gram[j][i] = sums[:, p : p + 1]
    weights = coefficients(gram, scale_ref[:, :1])
    total = weights[0] * vectors[0][...]
    for weight, ref in zip(weights[1:], vectors[1:]):
        total = total + weight * ref[...]
    out_ref[...] = total


def passed_along(value, axis, steps):
    count = lax.axis_size(axis)
    pairs = [(source, (source + steps) % count) for source in range(count)]
    return lax.ppermute(value, axis, pairs)


def exchange(value, name):
    axis, kind = name.split()
    if kind in ("up", "down"):
        return passed_along(value, axis, 1 if kind == "up" else -1)
    count = lax.axis_size(axis)
    ahead = 1 if kind == "later" else 0
    pairs = [(i, (i + (1 if i % 2 == ahead else -1)) % count) for i in range(count)]
    return lax.ppermute(value, axis, pairs)


def every(row, axis):
    count = row.shape[0]
    return lax.all_to_all(row.reshape(count, 1, 128), axis, 0, 0).reshape(count, 128)


def shape(*dims, dtype=F32):
    return jax.ShapeDtypeStruct(dims, dtype)


def call(kernel, out_shape, *args, scratch=(), flops=0, name=None, in_hbm=()):
    spaces = [pltpu.HBM if i in in_hbm else pltpu.VMEM for i in range(len(args))]
    args = [
        pltpu.with_memory_space_constraint(arg, space) if space == pltpu.HBM else arg
        for arg, space in zip(args, spaces)
    ]
    return pl.pallas_call(
        kernel,
        out_shape=out_shape,
        in_specs=[pl.BlockSpec(memory_space=space) for space in spaces],
        out_specs=jax.tree.map(lambda _: pl.BlockSpec(memory_space=pltpu.VMEM), out_shape),
        scratch_shapes=list(scratch),
        cost_estimate=pl.CostEstimate(flops=flops, bytes_accessed=4 * 1024 * 1024, transcendentals=0),
        compiler_params=pltpu.CompilerParams(vmem_limit_bytes=VMEM_BYTES),
        name=name,
    )(*args)


def per_device(
    right_side, face_table, send_faces, stabilize, coupling, inverse, lifting, trace_block
):
    source = right_side[0, 0]
    table = face_table[0, 0]
    send_lists = send_faces[0, 0]
    penalty = stabilize[0]
    scaling = coupling[0]
    dofs, owned = source.shape
    elements = table.shape[1]
    shared = send_lists.shape[1]
    faces = owned + 2 * shared
    shapes, trace, _ = lifting.shape
    part = shape(dofs, shared)

    slab, section, send_lists = call(
        first_kernel,
        (part, part, shape(*send_lists.shape, dtype=jnp.int32)),
        source,
        send_lists,
        scratch=[pltpu.VMEM(source.shape, F32), pltpu.SemaphoreType.DMA((2,))],
        name="first",
        in_hbm=(0, 1),
    )
    ghosts = [passed_along(section, "yz", 1), passed_along(slab, "gx", 1)]
    turned = jnp.swapaxes(lifting, 1, 2)
    select, spread, meet, leave, place, inverse, turned, trace_block = call(
        functools.partial(tables_kernel, shapes),
        (
            pltpu.VMEM((faces, 4 * elements), BF16),
            pltpu.VMEM((4 * elements, owned), BF16),
            pltpu.VMEM((4 * shared, 4 * elements), BF16),
            pltpu.VMEM((4 * elements, 4 * shared), BF16),
            shape(2 * shared, owned, dtype=BF16),
            shape(*inverse.shape),
            shape(*turned.shape),
            shape(*trace_block.shape),
        ),
        table,
        inverse,
        turned,
        trace_block,
        send_lists,
        scratch=[pltpu.VMEM(table.shape, jnp.int32), pltpu.SemaphoreType.DMA((4,))],
        flops=10**9,
        name="tables",
        in_hbm=(0, 1, 2, 3),
    )
    weights, scale = call(
        weights_kernel,
        (shape(shapes, 2 * trace, 3 * trace, dtype=BF16), shape(1, 128)),
        inverse,
        turned,
        trace_block,
        scratch=[pltpu.VMEM((8 * shapes, trace, 128), F32)],
        flops=10**9,
        name="weights",
    )
    odd = jnp.broadcast_to(
        jnp.stack([lax.axis_index("gx"), lax.axis_index("yz")])[:, None] % 2, (2, 128)
    ).astype(jnp.int32)
    known = call(gather_kernel, shape(dofs, 4 * elements), source, select, flops=10**9, name="gather")
    vectors = [source]
    grams = []
    own, got, sent = source, ghosts, [slab, section]
    along_yz = []
    ghost_sums = None
    both = shape(dofs, 2 * shared)
    for j in range(ITERS):
        first, final = j == 0, j == ITERS - 1
        outs = [shape(2 * dofs, 4 * elements, dtype=BF16)]
        results = call(
            functools.partial(step_kernel, first, final),
            tuple(outs + ([part] * 2 if final else [both] * 2 + [part] * 4)),
            known,
            *got,
            *sent,
            meet,
            leave,
            weights,
            penalty,
            scaling,
            scale,
            odd,
            flops=10**9,
            name=f"step{j}",
        )
        result = results[0]
        if final:
            after = [passed_along(results[1], "gx", -1), passed_along(results[2], "yz", 1)]
        else:
            down, sent = results[1], [results[2]]
            after = [exchange(value, name) for value, name in zip(results[3:], STARTS)]
        earlier = vectors[:j] if j else []
        outs = [shape(8, 128), shape(dofs, owned)]
        if not first:
            outs = [shape(dofs, owned)] + outs
        outs = outs + [part if final else shape(dofs, 4 * elements)]
        results = list(
            call(
                functools.partial(between_kernel, first, final, len(earlier)),
                tuple(outs),
                result,
                own,
                *([] if first else got),
                *([] if final else [down]),
                *earlier,
                select,
                spread,
                place,
                scale,
                odd,
                *([leave] if final else []),
                flops=10**9,
                name=f"between{j}",
            )
        )
        if not first:
            vectors.append(results.pop(0))
        grams.append(results.pop(0))
        own = results.pop(0)
        known = results.pop(0)
        along_yz += [got[0]] if first else [got[STARTS.index("yz up")], ghost_sums]
        ghost_sums = down
        got = after
    gx, yz = lax.axis_size("gx"), lax.axis_size("yz")
    rows = call(
        last_kernel,
        shape(yz, 128),
        own,
        *got,
        known,
        *vectors,
        *grams,
        *along_yz,
        place,
        scratch=[pltpu.VMEM((16, 128), F32)],
        name="last",
    )
    rows = call(add_kernel, shape(gx, 128), every(rows, "yz"), name="add")
    solution = call(solve_kernel, shape(dofs, owned), every(rows, "gx"), scale, *vectors, name="solve")
    return solution[None, None]


def solution(mesh):
    return jax.shard_map(
        per_device,
        mesh=mesh,
        in_specs=(
            P("gx", "yz", None, None),
            P("gx", "yz", None, None),
            P("gx", "yz", None, None),
            P("gx", "yz", None),
            P("gx", "yz", None),
            P(),
            P(),
            P(),
        ),
        out_specs=P("gx", "yz", None, None),
        check_vma=False,
    )
```

```python
import functools

import jax
import jax.numpy as jnp
from jax import lax
from jax.experimental import pallas as pl
from jax.experimental.pallas import tpu as pltpu
from jax.sharding import PartitionSpec as P

ITERS = 4
EPSILON = 1e-06
SHIFT = 12.0
NORM_ROOM = 1024.0
F32 = jnp.float32
BF16 = jnp.bfloat16
STARTS = ("gx later", "gx first", "yz up", "yz down")
PAIRS = [(i, j) for j in range(ITERS + 1) for i in range(j + 1)]
VMEM_BYTES = 20 * 1024 * 1024


def halves(value):
    high = value.astype(BF16)
    return high, (value - high.astype(F32)).astype(BF16)


def stacked(value):
    return jnp.concatenate(halves(value), axis=0)


def folded(value):
    half = value.shape[0] // 2
    return value[:half] + value[half:]


def dot(first, second):
    return jnp.dot(first, second, preferred_element_type=F32)


def dot_last(first, second, precision=None):
    return lax.dot_general(
        first, second, (((1,), (1,)), ((), ())), preferred_element_type=F32, precision=precision
    )


def fetched(sources, targets, semaphores):
    copies = [
        pltpu.make_async_copy(source, target, semaphores.at[k])
        for k, (source, target) in enumerate(zip(sources, targets))
    ]
    for copy in copies:
        copy.start()
    return [copy.wait for copy in copies]


def first_kernel(source_hbm, send_hbm, slab_ref, section_ref, send_ref, source_ref, semaphores):
    have_send, have_source = fetched((send_hbm, source_hbm), (send_ref, source_ref), semaphores)
    owned = source_ref.shape[1]
    shared = send_ref.shape[1]
    faces = lax.broadcasted_iota(jnp.int32, (owned, shared), 0)
    have_send()
    pick = jnp.concatenate(
        [jnp.where(faces == send_ref[row : row + 1, :], 1.0, 0.0).astype(BF16) for row in range(2)], axis=1
    )
    have_source()
    sent = folded(dot(stacked(source_ref[...]), pick))
    slab_ref[...] = sent[:, :shared]
    section_ref[...] = sent[:, shared:]


def three_pass(first, second):
    return dot_last(first[0], second[0]) + (dot_last(first[0], second[1]) + dot_last(first[1], second[0]))


def by_face(value, rows_ref, slot):
    rows, columns = value.shape
    parts = []
    for start in range(0, columns, 128):
        width = min(128, columns - start)
        rows_ref[slot, :, :width] = value[:, start : start + width]
        part = jnp.concatenate([rows_ref[slot, pl.ds(k, rows // 4, stride=4), :] for k in range(4)], axis=0)
        parts.append(part[:, :width])
        slot += 1
    return jnp.concatenate(parts, axis=1)


def columns(table_ref):
    table = table_ref[...].astype(F32)
    return jnp.concatenate([table, jnp.zeros((8 - table.shape[0], table.shape[1]), F32)], axis=0).T


def split_index(index):
    block = index // 128
    return block.astype(F32).astype(BF16), (index - block * 128).astype(F32).astype(BF16)


def tables_kernel(
    shapes, table_hbm, inverse_hbm, lifting_hbm, block_hbm, send_ref,
    select_ref, spread_ref, meet_ref, leave_ref, place_ref, inverse_ref, lifting_ref, block_ref, table_ref, semaphores,
):
    have_table, *have_weights = fetched(
        (table_hbm, block_hbm, lifting_hbm, inverse_hbm), (table_ref, block_ref, lifting_ref, inverse_ref), semaphores
    )
    faces = select_ref.shape[0]
    elements = table_ref.shape[1]
    sends = columns(send_ref)
    shared, owned = sends.shape[0], place_ref.shape[1]
    lanes = lax.broadcasted_iota(jnp.int32, (shared, owned), 1).astype(F32)
    for row in range(2):
        place_ref[row * shared : (row + 1) * shared, :] = jnp.where(
            sends[:, row : row + 1] == lanes, 1.0, 0.0
        ).astype(BF16)
    group = elements // shapes
    have_table()
    block, place_in = split_index(table_ref[...])
    table = table_ref[...].astype(F32)
    down = lax.broadcasted_iota(jnp.int32, (128, group), 0).astype(F32).astype(BF16)
    one, zero = jnp.ones((), BF16), jnp.zeros((), BF16)
    for t in range(shapes):
        part = slice(t * group, (t + 1) * group)
        for k in range(4):
            start = (t * 4 + k) * group
            in_block = jnp.broadcast_to(block[k : k + 1, part], (128, group))
            hit = jnp.where(jnp.broadcast_to(place_in[k : k + 1, part], (128, group)) == down, one, zero)
            for b in range(faces // 128):
                select_ref[b * 128 : (b + 1) * 128, start : start + group] = jnp.where(
                    in_block == jnp.full((), b, BF16), hit, zero
                )
            spread_ref[start : start + group, :] = select_ref[:owned, start : start + group].T
            row = table[k : k + 1, part]
            for i in range(2):
                meet_ref[2 * i * shared : (2 * i + 1) * shared, start : start + group] = jnp.where(
                    sends[:, i : i + 1] == row, 1.0, 0.0
                ).astype(BF16)
                meet_ref[(2 * i + 1) * shared : (2 * i + 2) * shared, start : start + group] = select_ref[
                    owned + i * shared : owned + (i + 1) * shared, start : start + group
                ]
            leave_ref[start : start + group, :] = meet_ref[:, start : start + group].T
    for have in have_weights:
        have()


def weights_kernel(inverse_ref, lifting_ref, block_ref, weight_ref, scale_ref, rows_ref):
    shapes = block_ref.shape[0]
    block_bound = jnp.zeros((1, 1), F32)
    inner_bound = jnp.zeros((1, 1), F32)
    for t in range(shapes):
        lifted = halves(by_face(lifting_ref[t].T, rows_ref, 8 * t))
        inner = three_pass(halves(three_pass(lifted, halves(inverse_ref[t]))), lifted)
        block = by_face(by_face(block_ref[t], rows_ref, 8 * t + 2).T, rows_ref, 8 * t + 5)
        block_bound = jnp.maximum(block_bound, jnp.sum(block * block, keepdims=True))
        inner_bound = jnp.maximum(inner_bound, jnp.sum(inner * inner, keepdims=True))
        high, low = halves(jnp.concatenate([block, inner], axis=0))
        weight_ref[t] = jnp.concatenate([high, high, low], axis=1)
    bound = 4.0 * (6.0 + jnp.sqrt(block_bound) + 2.0 * jnp.sqrt(inner_bound)) + SHIFT
    scale_ref[...] = jnp.broadcast_to(
        jnp.maximum(1.0, bound * (1.0 / NORM_ROOM)), scale_ref.shape
    )


def inner_products(vectors, last, gram_ref, first_row):
    for i, vector in enumerate(vectors):
        gram_ref[first_row + i : first_row + i + 1, :] = lane_sums(vector * last)


def lane_sums(product):
    total = product[:, :128]
    for start in range(128, product.shape[1], 128):
        total = total + product[:, start : start + 128]
    return jnp.sum(total, axis=0, keepdims=True)


def arrived(got, odd):
    parts = dict(zip(STARTS, [ref[...] for ref in got]))
    back = [jnp.where(odd, parts["gx later"], parts["gx first"]), parts["yz down"]]
    up = [jnp.where(odd, parts["gx first"], parts["gx later"]), parts["yz up"]]
    return back, up


def gather_kernel(source_ref, select_ref, known_ref):
    known_ref[...] = folded(dot(stacked(source_ref[...]), select_ref[: source_ref.shape[1], :]))


def partway_kernel(known_ref, later_ref, first_ref, meet_ref, odd_ref, read_ref):
    odd = odd_ref[:1, :] != 0
    later, first = later_ref[...], first_ref[...]
    pair = jnp.concatenate([jnp.where(odd, later, first), jnp.where(odd, first, later)], axis=1)
    rows = meet_ref.shape[0] // 2
    read_ref[...] = known_ref[...] + folded(dot(stacked(pair), meet_ref[:rows, :]))


def step_kernel(first, final, *refs):
    refs = list(refs)
    known_ref = refs.pop(0)
    got = [refs.pop(0) for _ in range(2 if first else 4)]
    sent_before = [refs.pop(0) for _ in range(2 if first else 1)]
    meet_ref, leave_ref, weight_ref, stabilize_ref, coupling_ref, scale_ref, odd_ref = refs[:7]
    result_ref = refs[7]
    odd = odd_ref[:1, :] != 0
    dofs = known_ref.shape[0]
    shared = leave_ref.shape[1] // 4
    shapes = weight_ref.shape[0]
    group = stabilize_ref.shape[1] // shapes
    trace = 4 * dofs

    own = jnp.concatenate([ref[...] for ref in sent_before], axis=1)
    if first:
        section, slab = [ref[...] for ref in got]
        read = folded(dot(stacked(slab), meet_ref[shared : 2 * shared, :]))
        read = read + folded(dot(stacked(section), meet_ref[3 * shared :, :]))
    else:
        back, up = arrived(got, odd)
        own = own + jnp.concatenate(back, axis=1)
        read = folded(dot(stacked(jnp.concatenate([back[1], up[1]], axis=1)), meet_ref[2 * shared :, :]))
    read = known_ref[...] + read
    for t in range(shapes):
        columns = slice(t * group, (t + 1) * group)
        values = jnp.concatenate(
            [read[:, (t * 4 + k) * group : (t * 4 + k + 1) * group] for k in range(4)], axis=0
        )
        high, low = halves(values)
        product = dot(weight_ref[t], jnp.concatenate([high, low, high], axis=0))
        result = (
            stabilize_ref[:, columns] * values + product[:trace] - product[trace:] / coupling_ref[:, columns]
        )
        for k in range(4):
            start = (t * 4 + k) * group
            result_ref[:, start : start + group] = stacked(result[k * dofs : (k + 1) * dofs])
    shrink = 1.0 / scale_ref[:, :1]
    if final:
        leaving = folded(dot(result_ref[...], leave_ref[:, shared : 3 * shared])) * shrink
        refs[8][...] = leaving[:, :shared]
        refs[9][...] = leaving[:, shared:] - (SHIFT * shrink) * own[:, shared:]
        return
    down_ref, sent_ref = refs[8:10]
    leaving = folded(dot(result_ref[...], leave_ref[...])) * shrink
    quarters = [leaving[:, i * shared : (i + 1) * shared] for i in range(4)]
    down = quarters[1::2]
    down_ref[...] = jnp.concatenate(down, axis=1)
    sent = jnp.concatenate(quarters[::2], axis=1) - (SHIFT * shrink) * own
    sent_ref[...] = sent
    up = [sent[:, i * shared : (i + 1) * shared] for i in range(2)]
    parts = {
        "gx later": jnp.where(odd, up[0], down[0]),
        "gx first": jnp.where(odd, down[0], up[0]),
        "yz up": up[1],
        "yz down": down[1],
    }
    for name, ref in zip(STARTS, refs[10:]):
        ref[...] = parts[name]


def between_kernel(first, final, earlier, *refs):
    refs = list(refs)
    result_ref, own_ref = refs[:2]
    refs = refs[2:]
    if not first:
        got, refs = refs[:4], refs[4:]
    if not final:
        down_ref = refs.pop(0)
    vectors, refs = refs[:earlier], refs[earlier:]
    select_ref, spread_ref, place_ref, scale_ref, odd_ref = refs[:5]
    refs = refs[5:]
    if final:
        leave_ref = refs.pop(0)
    if first:
        vector = own_ref[...]
    else:
        back, _ = arrived(got, odd_ref[:1, :] != 0)
        vector = own_ref[...] + folded(dot(stacked(jnp.concatenate(back, axis=1)), place_ref[...]))
        refs.pop(0)[...] = vector
    gram_ref, part_ref = refs[:2]
    shrink = 1.0 / scale_ref[:, :1]
    part = folded(dot(result_ref[...], spread_ref[...])) * shrink - (SHIFT * shrink) * vector
    part_ref[...] = part
    if final:
        ghost = leave_ref[:, 3 * leave_ref.shape[1] // 4 :]
        refs[2][...] = folded(dot(result_ref[...], ghost)) * shrink
    else:
        refs[2][...] = folded(dot(stacked(jnp.concatenate([part, down_ref[...]], axis=1)), select_ref[...]))
    inner_products([ref[...] for ref in vectors] + [vector], vector, gram_ref, 0)
    gram_ref[earlier + 1 :, :] = jnp.zeros((8 - earlier - 1, 128), F32)


def last_kernel(*refs):
    refs = list(refs)
    own_ref, slab_ref, section_ref, ghost_ref = [refs.pop(0) for _ in range(4)]
    vectors = [refs.pop(0) for _ in range(ITERS)]
    grams = [refs.pop(0) for _ in range(ITERS)]
    ghosts = [refs.pop(0)[...]]
    for _ in range(1, ITERS):
        arrived_ref, sums_ref = refs.pop(0), refs.pop(0)
        shared = arrived_ref.shape[1]
        ghosts.append(arrived_ref[...] + sums_ref[:, shared:])
    place_ref, row_ref, sums_ref = refs
    vector = own_ref[...] + folded(dot(stacked(slab_ref[...]), place_ref[:shared, :]))
    sent_along_yz = jnp.sum(place_ref[shared:, :].astype(F32), axis=0, keepdims=True)
    vector = jnp.where(sent_along_yz > 0.5, 0.0, vector)
    ghost = ghost_ref[...] + section_ref[...]
    sums_ref[...] = jnp.zeros(sums_ref.shape, F32)
    for j in range(ITERS):
        start = j * (j + 1) // 2
        sums_ref[start : start + j + 1, :] = grams[j][: j + 1, :]
    start = ITERS * (ITERS + 1) // 2
    for i, (whole, part) in enumerate(zip([ref[...] for ref in vectors] + [vector], ghosts + [ghost])):
        sums_ref[start + i : start + i + 1, :] = lane_sums(whole * vector) + lane_sums(part * ghost)
    totals = jnp.sum(sums_ref[...], axis=1, keepdims=True)
    count = sums_ref.shape[0]
    diagonal = lax.broadcasted_iota(jnp.int32, (count, 128), 0) == lax.broadcasted_iota(
        jnp.int32, (count, 128), 1
    )
    row = jnp.sum(jnp.where(diagonal, totals, 0.0), axis=0, keepdims=True)
    row_ref[...] = jnp.broadcast_to(row, row_ref.shape)


def added(terms):
    terms = list(terms)
    while len(terms) > 1:
        terms = [a + b for a, b in zip(terms[::2], terms[1::2])] + terms[len(terms) // 2 * 2 :]
    return terms[0]


def least_squares(hessenberg, target):
    breadth = len(hessenberg)
    height = len(target)
    unit_columns = []
    triangle = {}
    shrink = {}
    for k in range(breadth):
        column = list(hessenberg[k])
        for i in range(k):
            triangle[i, k] = added(unit_columns[i][r] * column[r] for r in range(height))
            column = [column[r] - triangle[i, k] * unit_columns[i][r] for r in range(height)]
        square = added(c * c for c in column)
        shrink[k] = lax.rsqrt(square)
        unit_columns.append([c * shrink[k] for c in column])
    projected = [added(v[r] * target[r] for r in range(height)) for v in unit_columns]
    outcome = [None] * breadth
    for k in reversed(range(breadth)):
        running = projected[k]
        for i in range(k + 1, breadth):
            running = running - triangle[k, i] * outcome[i]
        outcome[k] = running * shrink[k]
    return outcome


def coefficients(gram, scale):
    size = ITERS + 1
    zero = jnp.zeros_like(scale)

    def inner(a, b):
        rows = [(x, row) for x, row in zip(a, gram) if x is not None]
        return added(x * added(y * g for y, g in zip(b, row) if y is not None) for x, row in rows)

    def plus(a, factor, b):
        out = []
        for x, y in zip(a, b):
            if y is None:
                out.append(x)
            else:
                out.append(factor * y if x is None else x + factor * y)
        return out

    square = gram[0][0] + EPSILON
    initial_norm = jnp.sqrt(square)
    krylov = [[lax.rsqrt(square)] + [None] * ITERS]
    columns = []
    for j in range(ITERS):
        shifted = [None] + [scale * c if c is not None else None for c in krylov[j][:-1]]
        fresh = plus(shifted, SHIFT, krylov[j])
        products = [inner(vector, fresh) for vector in krylov]
        for value, vector in zip(products, krylov):
            fresh = plus(fresh, -value, vector)
        square = jnp.maximum(inner(fresh, fresh), 0.0) + EPSILON
        columns.append(products + [jnp.sqrt(square)] + [zero] * (ITERS - 1 - j))
        shrink = lax.rsqrt(square)
        krylov.append([c * shrink if c is not None else None for c in fresh])
    combine = least_squares(columns, [initial_norm] + [zero] * ITERS)
    total = [None] * size
    for y, vector in zip(combine, krylov):
        total = plus(total, y, vector)
    return total[:ITERS]


def add_kernel(rows_ref, out_ref):
    total = jnp.sum(rows_ref[...], axis=0, keepdims=True)
    out_ref[...] = jnp.broadcast_to(total, out_ref.shape)


def solve_kernel(rows_ref, scale_ref, *refs):
    vectors = refs[:ITERS]
    out_ref = refs[ITERS]
    sums = jnp.sum(rows_ref[...], axis=0, keepdims=True)
    gram = [[None] * (ITERS + 1) for _ in range(ITERS + 1)]
    for p, (i, j) in enumerate(PAIRS):
        gram[i][j] = gram[j][i] = sums[:, p : p + 1]
    weights = coefficients(gram, scale_ref[:, :1])
    total = weights[0] * vectors[0][...]
    for weight, ref in zip(weights[1:], vectors[1:]):
        total = total + weight * ref[...]
    out_ref[...] = total


def passed_along(value, axis, steps):
    count = lax.axis_size(axis)
    pairs = [(source, (source + steps) % count) for source in range(count)]
    return lax.ppermute(value, axis, pairs)


def exchange(value, name):
    axis, kind = name.split()
    if kind in ("up", "down"):
        return passed_along(value, axis, 1 if kind == "up" else -1)
    count = lax.axis_size(axis)
    ahead = 1 if kind == "later" else 0
    pairs = [(i, (i + (1 if i % 2 == ahead else -1)) % count) for i in range(count)]
    return lax.ppermute(value, axis, pairs)


def every(row, axis):
    count = row.shape[0]
    return lax.all_to_all(row.reshape(count, 1, 128), axis, 0, 0).reshape(count, 128)


def shape(*dims, dtype=F32):
    return jax.ShapeDtypeStruct(dims, dtype)


def call(kernel, out_shape, *args, scratch=(), flops=0, name=None, in_hbm=()):
    spaces = [pltpu.HBM if i in in_hbm else pltpu.VMEM for i in range(len(args))]
    args = [
        pltpu.with_memory_space_constraint(arg, space) if space == pltpu.HBM else arg
        for arg, space in zip(args, spaces)
    ]
    return pl.pallas_call(
        kernel,
        out_shape=out_shape,
        in_specs=[pl.BlockSpec(memory_space=space) for space in spaces],
        out_specs=jax.tree.map(lambda _: pl.BlockSpec(memory_space=pltpu.VMEM), out_shape),
        scratch_shapes=list(scratch),
        cost_estimate=pl.CostEstimate(flops=flops, bytes_accessed=4 * 1024 * 1024, transcendentals=0),
        compiler_params=pltpu.CompilerParams(vmem_limit_bytes=VMEM_BYTES),
        name=name,
    )(*args)


def per_device(
    right_side, face_table, send_faces, stabilize, coupling, inverse, lifting, trace_block
):
    source = right_side[0, 0]
    table = face_table[0, 0]
    send_lists = send_faces[0, 0]
    penalty = stabilize[0]
    scaling = coupling[0]
    dofs, owned = source.shape
    elements = table.shape[1]
    shared = send_lists.shape[1]
    faces = owned + 2 * shared
    shapes, trace, _ = lifting.shape
    part = shape(dofs, shared)

    slab, section, send_lists = call(
        first_kernel,
        (part, part, shape(*send_lists.shape, dtype=jnp.int32)),
        source,
        send_lists,
        scratch=[pltpu.VMEM(source.shape, F32), pltpu.SemaphoreType.DMA((2,))],
        name="first",
        in_hbm=(0, 1),
    )
    ghosts = [passed_along(section, "yz", 1), passed_along(slab, "gx", 1)]
    turned = jnp.swapaxes(lifting, 1, 2)
    select, spread, meet, leave, place, inverse, turned, trace_block = call(
        functools.partial(tables_kernel, shapes),
        (
            pltpu.VMEM((faces, 4 * elements), BF16),
            pltpu.VMEM((4 * elements, owned), BF16),
            pltpu.VMEM((4 * shared, 4 * elements), BF16),
            pltpu.VMEM((4 * elements, 4 * shared), BF16),
            shape(2 * shared, owned, dtype=BF16),
            shape(*inverse.shape),
            shape(*turned.shape),
            shape(*trace_block.shape),
        ),
        table,
        inverse,
        turned,
        trace_block,
        send_lists,
        scratch=[pltpu.VMEM(table.shape, jnp.int32), pltpu.SemaphoreType.DMA((4,))],
        flops=10**9,
        name="tables",
        in_hbm=(0, 1, 2, 3),
    )
    weights, scale = call(
        weights_kernel,
        (shape(shapes, 2 * trace, 3 * trace, dtype=BF16), shape(1, 128)),
        inverse,
        turned,
        trace_block,
        scratch=[pltpu.VMEM((8 * shapes, trace, 128), F32)],
        flops=10**9,
        name="weights",
    )
    odd = jnp.broadcast_to(
        jnp.stack([lax.axis_index("gx"), lax.axis_index("yz")])[:, None] % 2, (2, 128)
    ).astype(jnp.int32)
    known = call(gather_kernel, shape(dofs, 4 * elements), source, select, flops=10**9, name="gather")
    vectors = [source]
    grams = []
    own, got, sent = source, ghosts, [slab, section]
    along_yz = []
    ghost_sums = None
    both = shape(dofs, 2 * shared)
    for j in range(ITERS):
        first, final = j == 0, j == ITERS - 1
        outs = [shape(2 * dofs, 4 * elements, dtype=BF16)]
        if not first:
            along_gx = [got[STARTS.index(name)] for name in ("gx later", "gx first")]
            known = call(
                partway_kernel, shape(dofs, 4 * elements), known, *along_gx, meet, odd, flops=10**8, name=f"partway{j}"
            )
        results = call(
            functools.partial(step_kernel, first, final),
            tuple(outs + ([part] * 2 if final else [both] * 2 + [part] * 4)),
            known,
            *got,
            *sent,
            meet,
            leave,
            weights,
            penalty,
            scaling,
            scale,
            odd,
            flops=10**9,
            name=f"step{j}",
        )
        result = results[0]
        if final:
            after = [passed_along(results[1], "gx", -1), passed_along(results[2], "yz", 1)]
        else:
            down, sent = results[1], [results[2]]
            after = [exchange(value, name) for value, name in zip(results[3:], STARTS)]
        earlier = vectors[:j] if j else []
        outs = [shape(8, 128), shape(dofs, owned)]
        if not first:
            outs = [shape(dofs, owned)] + outs
        outs = outs + [part if final else shape(dofs, 4 * elements)]
        results = list(
            call(
                functools.partial(between_kernel, first, final, len(earlier)),
                tuple(outs),
                result,
                own,
                *([] if first else got),
                *([] if final else [down]),
                *earlier,
                select,
                spread,
                place,
                scale,
                odd,
                *([leave] if final else []),
                flops=10**9,
                name=f"between{j}",
            )
        )
        if not first:
            vectors.append(results.pop(0))
        grams.append(results.pop(0))
        own = results.pop(0)
        known = results.pop(0)
        along_yz += [got[0]] if first else [got[STARTS.index("yz up")], ghost_sums]
        ghost_sums = down
        got = after
    gx, yz = lax.axis_size("gx"), lax.axis_size("yz")
    rows = call(
        last_kernel,
        shape(yz, 128),
        own,
        *got,
        known,
        *vectors,
        *grams,
        *along_yz,
        place,
        scratch=[pltpu.VMEM((16, 128), F32)],
        name="last",
    )
    rows = call(add_kernel, shape(gx, 128), every(rows, "yz"), name="add")
    solution = call(solve_kernel, shape(dofs, owned), every(rows, "gx"), scale, *vectors, name="solve")
    return solution[None, None]


def solution(mesh):
    return jax.shard_map(
        per_device,
        mesh=mesh,
        in_specs=(
            P("gx", "yz", None, None),
            P("gx", "yz", None, None),
            P("gx", "yz", None, None),
            P("gx", "yz", None),
            P("gx", "yz", None),
            P(),
            P(),
            P(),
        ),
        out_specs=P("gx", "yz", None, None),
        check_vma=False,
    )
```

```python
import functools

import jax
import jax.numpy as jnp
from jax import lax
from jax.experimental import pallas as pl
from jax.experimental.pallas import tpu as pltpu
from jax.sharding import PartitionSpec as P

ITERS = 4
EPSILON = 1e-06
SHIFT = 12.0
NORM_ROOM = 1024.0
F32 = jnp.float32
BF16 = jnp.bfloat16
STARTS = ("gx later", "yz up", "gx first", "yz down")
PAIRS = [(i, j) for j in range(ITERS + 1) for i in range(j + 1)]
VMEM_BYTES = 20 * 1024 * 1024


def halves(value):
    high = value.astype(BF16)
    return high, (value - high.astype(F32)).astype(BF16)


def stacked(value):
    return jnp.concatenate(halves(value), axis=0)


def folded(value):
    half = value.shape[0] // 2
    return value[:half] + value[half:]


def dot(first, second):
    return jnp.dot(first, second, preferred_element_type=F32)


def dot_last(first, second, precision=None):
    return lax.dot_general(
        first, second, (((1,), (1,)), ((), ())), preferred_element_type=F32, precision=precision
    )


def fetched(sources, targets, semaphores):
    copies = [
        pltpu.make_async_copy(source, target, semaphores.at[k])
        for k, (source, target) in enumerate(zip(sources, targets))
    ]
    for copy in copies:
        copy.start()
    return [copy.wait for copy in copies]


def first_kernel(source_hbm, send_hbm, slab_ref, section_ref, send_ref, source_ref, semaphores):
    have_send, have_source = fetched((send_hbm, source_hbm), (send_ref, source_ref), semaphores)
    owned = source_ref.shape[1]
    shared = send_ref.shape[1]
    faces = lax.broadcasted_iota(jnp.int32, (owned, shared), 0)
    have_send()
    pick = jnp.concatenate(
        [jnp.where(faces == send_ref[row : row + 1, :], 1.0, 0.0).astype(BF16) for row in range(2)], axis=1
    )
    have_source()
    sent = folded(dot(stacked(source_ref[...]), pick))
    slab_ref[...] = sent[:, :shared]
    section_ref[...] = sent[:, shared:]


def three_pass(first, second):
    return dot_last(first[0], second[0]) + (dot_last(first[0], second[1]) + dot_last(first[1], second[0]))


def by_face(value, rows_ref, slot):
    rows, columns = value.shape
    parts = []
    for start in range(0, columns, 128):
        width = min(128, columns - start)
        rows_ref[slot, :, :width] = value[:, start : start + width]
        part = jnp.concatenate([rows_ref[slot, pl.ds(k, rows // 4, stride=4), :] for k in range(4)], axis=0)
        parts.append(part[:, :width])
        slot += 1
    return jnp.concatenate(parts, axis=1)


def columns(table_ref):
    table = table_ref[...].astype(F32)
    return jnp.concatenate([table, jnp.zeros((8 - table.shape[0], table.shape[1]), F32)], axis=0).T


def split_index(index):
    block = index // 128
    return block.astype(F32).astype(BF16), (index - block * 128).astype(F32).astype(BF16)


def tables_kernel(
    shapes, table_hbm, inverse_hbm, lifting_hbm, block_hbm, send_ref,
    select_ref, spread_ref, meet_ref, leave_ref, place_ref, inverse_ref, lifting_ref, block_ref, table_ref, semaphores,
):
    have_table, *have_weights = fetched(
        (table_hbm, block_hbm, lifting_hbm, inverse_hbm), (table_ref, block_ref, lifting_ref, inverse_ref), semaphores
    )
    faces = select_ref.shape[0]
    elements = table_ref.shape[1]
    sends = columns(send_ref)
    shared, owned = sends.shape[0], place_ref.shape[1]
    lanes = lax.broadcasted_iota(jnp.int32, (shared, owned), 1).astype(F32)
    for row in range(2):
        place_ref[row * shared : (row + 1) * shared, :] = jnp.where(
            sends[:, row : row + 1] == lanes, 1.0, 0.0
        ).astype(BF16)
    group = elements // shapes
    have_table()
    block, place_in = split_index(table_ref[...])
    table = table_ref[...].astype(F32)
    down = lax.broadcasted_iota(jnp.int32, (128, group), 0).astype(F32).astype(BF16)
    one, zero = jnp.ones((), BF16), jnp.zeros((), BF16)
    for t in range(shapes):
        part = slice(t * group, (t + 1) * group)
        for k in range(4):
            start = (t * 4 + k) * group
            in_block = jnp.broadcast_to(block[k : k + 1, part], (128, group))
            hit = jnp.where(jnp.broadcast_to(place_in[k : k + 1, part], (128, group)) == down, one, zero)
            for b in range(faces // 128):
                select_ref[b * 128 : (b + 1) * 128, start : start + group] = jnp.where(
                    in_block == jnp.full((), b, BF16), hit, zero
                )
            spread_ref[start : start + group, :] = select_ref[:owned, start : start + group].T
            row = table[k : k + 1, part]
            for i in range(2):
                meet_ref[i * shared : (i + 1) * shared, start : start + group] = jnp.where(
                    sends[:, i : i + 1] == row, 1.0, 0.0
                ).astype(BF16)
            meet_ref[2 * shared :, start : start + group] = select_ref[owned:, start : start + group]
            leave_ref[start : start + group, :] = meet_ref[:, start : start + group].T
    for have in have_weights:
        have()


def weights_kernel(inverse_ref, lifting_ref, block_ref, weight_ref, scale_ref, rows_ref):
    shapes = block_ref.shape[0]
    block_bound = jnp.zeros((1, 1), F32)
    inner_bound = jnp.zeros((1, 1), F32)
    for t in range(shapes):
        lifted = halves(by_face(lifting_ref[t].T, rows_ref, 8 * t))
        inner = three_pass(halves(three_pass(lifted, halves(inverse_ref[t]))), lifted)
        block = by_face(by_face(block_ref[t], rows_ref, 8 * t + 2).T, rows_ref, 8 * t + 5)
        block_bound = jnp.maximum(block_bound, jnp.sum(block * block, keepdims=True))
        inner_bound = jnp.maximum(inner_bound, jnp.sum(inner * inner, keepdims=True))
        high, low = halves(jnp.concatenate([block, inner], axis=0))
        weight_ref[t] = jnp.concatenate([high, high, low], axis=1)
    bound = 4.0 * (6.0 + jnp.sqrt(block_bound) + 2.0 * jnp.sqrt(inner_bound)) + SHIFT
    scale_ref[...] = jnp.broadcast_to(
        jnp.maximum(1.0, bound * (1.0 / NORM_ROOM)), scale_ref.shape
    )


def inner_products(vectors, last, gram_ref, first_row):
    for i, vector in enumerate(vectors):
        gram_ref[first_row + i : first_row + i + 1, :] = lane_sums(vector * last)


def lane_sums(product):
    total = product[:, :128]
    for start in range(128, product.shape[1], 128):
        total = total + product[:, start : start + 128]
    return jnp.sum(total, axis=0, keepdims=True)


def arrived(got, odd):
    parts = dict(zip(STARTS, [ref[...] for ref in got]))
    back = [jnp.where(odd, parts["gx later"], parts["gx first"]), parts["yz down"]]
    up = [jnp.where(odd, parts["gx first"], parts["gx later"]), parts["yz up"]]
    return back, up


def gather_kernel(source_ref, select_ref, known_ref):
    known_ref[...] = folded(dot(stacked(source_ref[...]), select_ref[: source_ref.shape[1], :]))


def step_kernel(first, final, *refs):
    refs = list(refs)
    known_ref = refs.pop(0)
    got = [refs.pop(0) for _ in range(2 if first else 4)]
    sent_before = [refs.pop(0) for _ in range(2 if first else 1)]
    meet_ref, leave_ref, weight_ref, stabilize_ref, coupling_ref, scale_ref, odd_ref = refs[:7]
    result_ref = refs[7]
    odd = odd_ref[:1, :] != 0
    dofs = known_ref.shape[0]
    shared = leave_ref.shape[1] // 4
    shapes = weight_ref.shape[0]
    group = stabilize_ref.shape[1] // shapes
    trace = 4 * dofs

    own = jnp.concatenate([ref[...] for ref in sent_before], axis=1)
    if first:
        section, slab = [ref[...] for ref in got]
        arrivals = jnp.concatenate([slab, section], axis=1)
        read = folded(dot(stacked(arrivals), meet_ref[2 * shared :, :]))
    else:
        back, up = arrived(got, odd)
        own = own + jnp.concatenate(back, axis=1)
        read = folded(dot(stacked(jnp.concatenate(back + up, axis=1)), meet_ref[...]))
    read = known_ref[...] + read
    for t in range(shapes):
        columns = slice(t * group, (t + 1) * group)
        values = jnp.concatenate(
            [read[:, (t * 4 + k) * group : (t * 4 + k + 1) * group] for k in range(4)], axis=0
        )
        high, low = halves(values)
        product = dot(weight_ref[t], jnp.concatenate([high, low, high], axis=0))
        result = (
            stabilize_ref[:, columns] * values + product[:trace] - product[trace:] / coupling_ref[:, columns]
        )
        for k in range(4):
            start = (t * 4 + k) * group
            result_ref[:, start : start + group] = stacked(result[k * dofs : (k + 1) * dofs])
    shrink = 1.0 / scale_ref[:, :1]
    if final:
        leaving = folded(dot(result_ref[...], leave_ref[:, shared : 3 * shared])) * shrink
        refs[8][...] = leaving[:, shared:]
        refs[9][...] = leaving[:, :shared] - (SHIFT * shrink) * own[:, shared:]
        return
    down_ref, sent_ref = refs[8:10]
    leaving = folded(dot(result_ref[...], leave_ref[...])) * shrink
    down = [leaving[:, (2 + i) * shared : (3 + i) * shared] for i in range(2)]
    down_ref[...] = leaving[:, 2 * shared :]
    sent = leaving[:, : 2 * shared] - (SHIFT * shrink) * own
    sent_ref[...] = sent
    up = [sent[:, i * shared : (i + 1) * shared] for i in range(2)]
    parts = {
        "gx later": jnp.where(odd, up[0], down[0]),
        "gx first": jnp.where(odd, down[0], up[0]),
        "yz up": up[1],
        "yz down": down[1],
    }
    for name, ref in zip(STARTS, refs[10:]):
        ref[...] = parts[name]


def between_kernel(first, final, earlier, *refs):
    refs = list(refs)
    result_ref, own_ref = refs[:2]
    refs = refs[2:]
    if not first:
        got, refs = refs[:4], refs[4:]
    if not final:
        down_ref = refs.pop(0)
    vectors, refs = refs[:earlier], refs[earlier:]
    select_ref, spread_ref, place_ref, scale_ref, odd_ref = refs[:5]
    refs = refs[5:]
    if final:
        leave_ref = refs.pop(0)
    if first:
        vector = own_ref[...]
    else:
        back, _ = arrived(got, odd_ref[:1, :] != 0)
        vector = own_ref[...] + folded(dot(stacked(jnp.concatenate(back, axis=1)), place_ref[...]))
        refs.pop(0)[...] = vector
    gram_ref, part_ref = refs[:2]
    shrink = 1.0 / scale_ref[:, :1]
    part = folded(dot(result_ref[...], spread_ref[...])) * shrink - (SHIFT * shrink) * vector
    part_ref[...] = part
    if final:
        ghost = leave_ref[:, 3 * leave_ref.shape[1] // 4 :]
        refs[2][...] = folded(dot(result_ref[...], ghost)) * shrink
    else:
        refs[2][...] = folded(dot(stacked(jnp.concatenate([part, down_ref[...]], axis=1)), select_ref[...]))
    inner_products([ref[...] for ref in vectors] + [vector], vector, gram_ref, 0)
    gram_ref[earlier + 1 :, :] = jnp.zeros((8 - earlier - 1, 128), F32)


def last_kernel(*refs):
    refs = list(refs)
    own_ref, slab_ref, section_ref, ghost_ref = [refs.pop(0) for _ in range(4)]
    vectors = [refs.pop(0) for _ in range(ITERS)]
    grams = [refs.pop(0) for _ in range(ITERS)]
    ghosts = [refs.pop(0)[...]]
    for _ in range(1, ITERS):
        arrived_ref, sums_ref = refs.pop(0), refs.pop(0)
        shared = arrived_ref.shape[1]
        ghosts.append(arrived_ref[...] + sums_ref[:, shared:])
    place_ref, row_ref, sums_ref = refs
    vector = own_ref[...] + folded(dot(stacked(slab_ref[...]), place_ref[:shared, :]))
    sent_along_yz = jnp.sum(place_ref[shared:, :].astype(F32), axis=0, keepdims=True)
    vector = jnp.where(sent_along_yz > 0.5, 0.0, vector)
    ghost = ghost_ref[...] + section_ref[...]
    sums_ref[...] = jnp.zeros(sums_ref.shape, F32)
    for j in range(ITERS):
        start = j * (j + 1) // 2
        sums_ref[start : start + j + 1, :] = grams[j][: j + 1, :]
    start = ITERS * (ITERS + 1) // 2
    for i, (whole, part) in enumerate(zip([ref[...] for ref in vectors] + [vector], ghosts + [ghost])):
        sums_ref[start + i : start + i + 1, :] = lane_sums(whole * vector) + lane_sums(part * ghost)
    totals = jnp.sum(sums_ref[...], axis=1, keepdims=True)
    count = sums_ref.shape[0]
    diagonal = lax.broadcasted_iota(jnp.int32, (count, 128), 0) == lax.broadcasted_iota(
        jnp.int32, (count, 128), 1
    )
    row = jnp.sum(jnp.where(diagonal, totals, 0.0), axis=0, keepdims=True)
    row_ref[...] = jnp.broadcast_to(row, row_ref.shape)


def added(terms):
    terms = list(terms)
    while len(terms) > 1:
        terms = [a + b for a, b in zip(terms[::2], terms[1::2])] + terms[len(terms) // 2 * 2 :]
    return terms[0]


def least_squares(hessenberg, target):
    breadth = len(hessenberg)
    height = len(target)
    unit_columns = []
    triangle = {}
    shrink = {}
    for k in range(breadth):
        column = list(hessenberg[k])
        for i in range(k):
            triangle[i, k] = added(unit_columns[i][r] * column[r] for r in range(height))
            column = [column[r] - triangle[i, k] * unit_columns[i][r] for r in range(height)]
        square = added(c * c for c in column)
        shrink[k] = lax.rsqrt(square)
        unit_columns.append([c * shrink[k] for c in column])
    projected = [added(v[r] * target[r] for r in range(height)) for v in unit_columns]
    outcome = [None] * breadth
    for k in reversed(range(breadth)):
        running = projected[k]
        for i in range(k + 1, breadth):
            running = running - triangle[k, i] * outcome[i]
        outcome[k] = running * shrink[k]
    return outcome


def coefficients(gram, scale):
    size = ITERS + 1
    zero = jnp.zeros_like(scale)

    def inner(a, b):
        rows = [(x, row) for x, row in zip(a, gram) if x is not None]
        return added(x * added(y * g for y, g in zip(b, row) if y is not None) for x, row in rows)

    def plus(a, factor, b):
        out = []
        for x, y in zip(a, b):
            if y is None:
                out.append(x)
            else:
                out.append(factor * y if x is None else x + factor * y)
        return out

    square = gram[0][0] + EPSILON
    initial_norm = jnp.sqrt(square)
    krylov = [[lax.rsqrt(square)] + [None] * ITERS]
    columns = []
    for j in range(ITERS):
        shifted = [None] + [scale * c if c is not None else None for c in krylov[j][:-1]]
        fresh = plus(shifted, SHIFT, krylov[j])
        products = [inner(vector, fresh) for vector in krylov]
        for value, vector in zip(products, krylov):
            fresh = plus(fresh, -value, vector)
        square = jnp.maximum(inner(fresh, fresh), 0.0) + EPSILON
        columns.append(products + [jnp.sqrt(square)] + [zero] * (ITERS - 1 - j))
        shrink = lax.rsqrt(square)
        krylov.append([c * shrink if c is not None else None for c in fresh])
    combine = least_squares(columns, [initial_norm] + [zero] * ITERS)
    total = [None] * size
    for y, vector in zip(combine, krylov):
        total = plus(total, y, vector)
    return total[:ITERS]


def add_kernel(rows_ref, out_ref):
    total = jnp.sum(rows_ref[...], axis=0, keepdims=True)
    out_ref[...] = jnp.broadcast_to(total, out_ref.shape)


def solve_kernel(rows_ref, scale_ref, *refs):
    vectors = refs[:ITERS]
    out_ref = refs[ITERS]
    sums = jnp.sum(rows_ref[...], axis=0, keepdims=True)
    gram = [[None] * (ITERS + 1) for _ in range(ITERS + 1)]
    for p, (i, j) in enumerate(PAIRS):
        gram[i][j] = gram[j][i] = sums[:, p : p + 1]
    weights = coefficients(gram, scale_ref[:, :1])
    total = weights[0] * vectors[0][...]
    for weight, ref in zip(weights[1:], vectors[1:]):
        total = total + weight * ref[...]
    out_ref[...] = total


def passed_along(value, axis, steps):
    count = lax.axis_size(axis)
    pairs = [(source, (source + steps) % count) for source in range(count)]
    return lax.ppermute(value, axis, pairs)


def exchange(value, name):
    axis, kind = name.split()
    if kind in ("up", "down"):
        return passed_along(value, axis, 1 if kind == "up" else -1)
    count = lax.axis_size(axis)
    ahead = 1 if kind == "later" else 0
    pairs = [(i, (i + (1 if i % 2 == ahead else -1)) % count) for i in range(count)]
    return lax.ppermute(value, axis, pairs)


def every(row, axis):
    count = row.shape[0]
    return lax.all_to_all(row.reshape(count, 1, 128), axis, 0, 0).reshape(count, 128)


def shape(*dims, dtype=F32):
    return jax.ShapeDtypeStruct(dims, dtype)


def call(kernel, out_shape, *args, scratch=(), flops=0, name=None, in_hbm=()):
    spaces = [pltpu.HBM if i in in_hbm else pltpu.VMEM for i in range(len(args))]
    args = [
        pltpu.with_memory_space_constraint(arg, space) if space == pltpu.HBM else arg
        for arg, space in zip(args, spaces)
    ]
    return pl.pallas_call(
        kernel,
        out_shape=out_shape,
        in_specs=[pl.BlockSpec(memory_space=space) for space in spaces],
        out_specs=jax.tree.map(lambda _: pl.BlockSpec(memory_space=pltpu.VMEM), out_shape),
        scratch_shapes=list(scratch),
        cost_estimate=pl.CostEstimate(flops=flops, bytes_accessed=4 * 1024 * 1024, transcendentals=0),
        compiler_params=pltpu.CompilerParams(vmem_limit_bytes=VMEM_BYTES),
        name=name,
    )(*args)


def per_device(
    right_side, face_table, send_faces, stabilize, coupling, inverse, lifting, trace_block
):
    source = right_side[0, 0]
    table = face_table[0, 0]
    send_lists = send_faces[0, 0]
    penalty = stabilize[0]
    scaling = coupling[0]
    dofs, owned = source.shape
    elements = table.shape[1]
    shared = send_lists.shape[1]
    faces = owned + 2 * shared
    shapes, trace, _ = lifting.shape
    part = shape(dofs, shared)

    slab, section, send_lists = call(
        first_kernel,
        (part, part, shape(*send_lists.shape, dtype=jnp.int32)),
        source,
        send_lists,
        scratch=[pltpu.VMEM(source.shape, F32), pltpu.SemaphoreType.DMA((2,))],
        name="first",
        in_hbm=(0, 1),
    )
    ghosts = [passed_along(section, "yz", 1), passed_along(slab, "gx", 1)]
    turned = jnp.swapaxes(lifting, 1, 2)
    select, spread, meet, leave, place, inverse, turned, trace_block = call(
        functools.partial(tables_kernel, shapes),
        (
            pltpu.VMEM((faces, 4 * elements), BF16),
            pltpu.VMEM((4 * elements, owned), BF16),
            pltpu.VMEM((4 * shared, 4 * elements), BF16),
            pltpu.VMEM((4 * elements, 4 * shared), BF16),
            shape(2 * shared, owned, dtype=BF16),
            shape(*inverse.shape),
            shape(*turned.shape),
            shape(*trace_block.shape),
        ),
        table,
        inverse,
        turned,
        trace_block,
        send_lists,
        scratch=[pltpu.VMEM(table.shape, jnp.int32), pltpu.SemaphoreType.DMA((4,))],
        flops=10**9,
        name="tables",
        in_hbm=(0, 1, 2, 3),
    )
    weights, scale = call(
        weights_kernel,
        (shape(shapes, 2 * trace, 3 * trace, dtype=BF16), shape(1, 128)),
        inverse,
        turned,
        trace_block,
        scratch=[pltpu.VMEM((8 * shapes, trace, 128), F32)],
        flops=10**9,
        name="weights",
    )
    odd = jnp.broadcast_to(
        jnp.stack([lax.axis_index("gx"), lax.axis_index("yz")])[:, None] % 2, (2, 128)
    ).astype(jnp.int32)
    known = call(gather_kernel, shape(dofs, 4 * elements), source, select, flops=10**9, name="gather")
    vectors = [source]
    grams = []
    own, got, sent = source, ghosts, [slab, section]
    along_yz = []
    ghost_sums = None
    both = shape(dofs, 2 * shared)
    for j in range(ITERS):
        first, final = j == 0, j == ITERS - 1
        outs = [shape(2 * dofs, 4 * elements, dtype=BF16)]
        results = call(
            functools.partial(step_kernel, first, final),
            tuple(outs + ([part] * 2 if final else [both] * 2 + [part] * 4)),
            known,
            *got,
            *sent,
            meet,
            leave,
            weights,
            penalty,
            scaling,
            scale,
            odd,
            flops=10**9,
            name=f"step{j}",
        )
        result = results[0]
        if final:
            after = [passed_along(results[1], "gx", -1), passed_along(results[2], "yz", 1)]
        else:
            down, sent = results[1], [results[2]]
            after = [exchange(value, name) for value, name in zip(results[3:], STARTS)]
        earlier = vectors[:j] if j else []
        outs = [shape(8, 128), shape(dofs, owned)]
        if not first:
            outs = [shape(dofs, owned)] + outs
        outs = outs + [part if final else shape(dofs, 4 * elements)]
        results = list(
            call(
                functools.partial(between_kernel, first, final, len(earlier)),
                tuple(outs),
                result,
                own,
                *([] if first else got),
                *([] if final else [down]),
                *earlier,
                select,
                spread,
                place,
                scale,
                odd,
                *([leave] if final else []),
                flops=10**9,
                name=f"between{j}",
            )
        )
        if not first:
            vectors.append(results.pop(0))
        grams.append(results.pop(0))
        own = results.pop(0)
        known = results.pop(0)
        along_yz += [got[0]] if first else [got[STARTS.index("yz up")], ghost_sums]
        ghost_sums = down
        got = after
    gx, yz = lax.axis_size("gx"), lax.axis_size("yz")
    rows = call(
        last_kernel,
        shape(yz, 128),
        own,
        *got,
        known,
        *vectors,
        *grams,
        *along_yz,
        place,
        scratch=[pltpu.VMEM((16, 128), F32)],
        name="last",
    )
    rows = call(add_kernel, shape(gx, 128), every(rows, "yz"), name="add")
    solution = call(solve_kernel, shape(dofs, owned), every(rows, "gx"), scale, *vectors, name="solve")
    return solution[None, None]


def solution(mesh):
    return jax.shard_map(
        per_device,
        mesh=mesh,
        in_specs=(
            P("gx", "yz", None, None),
            P("gx", "yz", None, None),
            P("gx", "yz", None, None),
            P("gx", "yz", None),
            P("gx", "yz", None),
            P(),
            P(),
            P(),
        ),
        out_specs=P("gx", "yz", None, None),
        check_vma=False,
    )
```
